32 devices in a mesh: az: 16 (over z, y, core), rad: 2 (over x).
Axes of the slice: x: 2, y: 2, z: 4, core: 2. Of those that a mesh axis runs over, the one named last changes fastest.
Arguments:
- fluid_state: float32 [5, 2, 128, 2048], P(None, None, 'rad', 'az'), may hold values from -6 to 6
- velocity: float32 [2, 2, 128, 2048], P(None, None, 'rad', 'az'), may hold values from -0.4 to 0.4
- shifts: int32 [128], P('rad'), may hold values from 0 to 160, as said below
- fraction: float32 [128], P('rad'), may hold values from 0 to 1
Outputs:
- advected: float32 [5, 2, 128, 2048], P(None, None, 'rad', 'az')
The draws below stay inside these ranges and needn't reach their ends.
Inputs may be any that keep to these rules, and one draw needn't show every extreme that they name: `shifts`: in every draw some cycle has shift 160 and some cycle has shift 0.
All inputs are finite; a program needn't handle non-finite values.
Results may differ from the reference program's by a relative error of at most 0.00002.
Values sent between devices are 32-bit elements; how exact they have to be, the bound alone decides.
A program may use at most 64 MiB of HBM per device.

```python
import jax
import jax.numpy as jnp
from jax import lax

FIELDS = 5
LAYERS = 2
STEPS = 2
MAXSHIFT = 160
RADIUS = 128
AZIMUTH = 2048


def draw_shifts(key, part):
    pick_key, value_key = jax.random.split(key)
    values = jax.random.randint(value_key, (RADIUS,), 0, MAXSHIFT + 1, dtype=jnp.int32)
    ranking = jax.random.permutation(pick_key, RADIUS)
    values = values.at[ranking[0]].set(MAXSHIFT)
    values = values.at[ranking[1]].set(0)
    return values


def draw_velocity(key, part):
    sign_key, size_key = jax.random.split(jax.random.fold_in(key, 7))
    flips = jax.random.randint(sign_key, (2, LAYERS, RADIUS, AZIMUTH), 0, 2, dtype=jnp.int32)
    signs = (1 - 2 * flips).astype(jnp.float32)
    spread = jax.random.uniform(size_key, (2, LAYERS, RADIUS, AZIMUTH), jnp.float32, 0.0, 1.0)
    magnitude = 0.2 * jnp.exp(spread * jnp.log(2.0))
    return signs * magnitude


def block_scale(rng, shape, cuts, low, top_value):
    loudness = 1.0
    for axis_at, parts in cuts:
        draws = jax.random.uniform(jax.random.fold_in(jax.random.fold_in(rng, 6), axis_at), (parts,), jnp.float32, low / len(cuts), top_value / len(cuts))
        loudness = loudness * jnp.repeat(jnp.exp(draws), shape[axis_at] // parts).reshape((-1,) + (1,) * (len(shape) - 1 - axis_at))
    return loudness


def gaussian(rng, dims, scale, limit, cuts=(), held_as=jnp.bfloat16):
    array = jax.random.normal(rng, dims, jnp.float32) * scale
    if len(cuts) > 0:
        array = block_scale(rng, dims, cuts, -0.22, 0.18) * array
    return jnp.clip(array, min=-limit, max=limit).astype(held_as)


def setup_inputs(seed: int = 0) -> dict:
    seeds = jax.random.split(jax.random.key(seed), 5)
    fluid_state = gaussian(seeds[0], (FIELDS, LAYERS, RADIUS, AZIMUTH), 1.0, 6.0, ((2, 2), (3, 16)), jnp.float32)
    velocity = draw_velocity(jax.random.fold_in(seeds[4], 71), 0)
    shifts = draw_shifts(jax.random.fold_in(seeds[4], 71), 0)
    fraction = jnp.clip(1.0 * jax.random.uniform(seeds[3], (RADIUS,), jnp.float32) ** block_scale(seeds[3], (RADIUS,), ((0, 2),), -0.2, 0.2), 0.0, 1.0)
    return dict(fluid_state=fluid_state, velocity=velocity, shifts=shifts, fraction=fraction)


def wrap_pad(values, margin):
    wrapped = jnp.concatenate([values[..., -margin:], values, values[..., :margin]], axis=-1)
    widths = [(0, 0)] * (values.ndim - 2) + [(margin, margin), (0, 0)]
    return jnp.pad(wrapped, widths)


def tendency(padded, velocity_pad):
    radial_speed = velocity_pad[0]
    cycle_speed = velocity_pad[1]
    face_radial = 0.5 * (radial_speed[..., :-1, 1:-1] + radial_speed[..., 1:, 1:-1])
    flux_radial = jnp.maximum(face_radial, 0.0) * padded[..., :-1, 1:-1] + jnp.minimum(face_radial, 0.0) * padded[..., 1:, 1:-1]
    face_cycle = 0.5 * (cycle_speed[..., 1:-1, :-1] + cycle_speed[..., 1:-1, 1:])
    flux_cycle = jnp.maximum(face_cycle, 0.0) * padded[..., 1:-1, :-1] + jnp.minimum(face_cycle, 0.0) * padded[..., 1:-1, 1:]
    return -((flux_radial[..., 1:, :] - flux_radial[..., :-1, :]) + (flux_cycle[..., 1:] - flux_cycle[..., :-1]))


def reference(fluid_state, velocity, shifts, fraction):
    velocity_pad = wrap_pad(velocity, 1)
    columns = jnp.arange(AZIMUTH, dtype=jnp.int32)
    source = (columns[None, :] - shifts[:, None].astype(jnp.int32)) % AZIMUTH
    before = (source - 1) % AZIMUTH
    weight = fraction[None, :, None]

    def advance(values):
        for sweep_index in range(STEPS):
            sectioned = values + tendency(wrap_pad(values, 1), velocity_pad)
            values = 0.5 * (values + (sectioned + tendency(wrap_pad(sectioned, 1), velocity_pad)))
        leading = jnp.take_along_axis(values, jnp.broadcast_to(source[None], values.shape), axis=2)
        trailing = jnp.take_along_axis(values, jnp.broadcast_to(before[None], values.shape), axis=2)
        return (1.0 - weight) * leading + weight * trailing

    return lax.map(advance, fluid_state)
```

```python
import functools

import jax
import jax.numpy as jnp
from jax import lax
from jax.experimental import pallas as pl
from jax.experimental.pallas import tpu as pltpu
from jax.sharding import PartitionSpec as P

STEPS = 2
EDGE = 8


def kernel(
    n_az, n_rad, fields, layers,
    fluid, vel, shift_ref, frac_ref, out,
    xin, edge_lo, edge_hi, row_lo, row_hi, halo_l, halo_r, halo_d, halo_u,
    coef, rot, tail, got, got_tail, done,
    in_sem, send_h, recv_h, send_a, recv_a, send_b, recv_b, out_sem,
):
    slabs = fields * layers
    vels = 2 * layers
    total = slabs + vels
    rows, width = xin.shape[1], xin.shape[2]
    tall = rows + 2 * EDGE
    az = lax.axis_index("az")
    rad = lax.axis_index("rad")
    right = lax.rem(az + 1, n_az)
    right2 = lax.rem(az + 2, n_az)
    left = lax.rem(az + n_az - 1, n_az)
    left2 = lax.rem(az + n_az - 2, n_az)
    has_dn = rad > 0
    has_up = rad < n_rad - 1

    def dev(a, r):
        return {"az": a, "rad": r}

    load_f = pltpu.make_async_copy(fluid, xin.at[pl.ds(0, slabs)], in_sem.at[0])
    load_v = pltpu.make_async_copy(vel, xin.at[pl.ds(slabs, vels)], in_sem.at[1])
    load_f.start()
    load_v.start()

    barrier = pltpu.get_barrier_semaphore()
    for a in (left, right, left2):
        pl.semaphore_signal(barrier, inc=1, device_id=dev(a, rad))

    @pl.when(has_dn)
    def _():
        for a in (left, az, right):
            pl.semaphore_signal(barrier, inc=1, device_id=dev(a, rad - 1))

    @pl.when(has_up)
    def _():
        for a in (left, az, right):
            pl.semaphore_signal(barrier, inc=1, device_id=dev(a, rad + 1))

    sub8 = lax.broadcasted_iota(jnp.int32, (EDGE, width), 0)
    lane_r = lax.broadcasted_iota(jnp.int32, (rows, width), 1)
    row_r = lax.broadcasted_iota(jnp.int32, (rows, width), 0)
    lane_t = lax.broadcasted_iota(jnp.int32, (tall, width), 1)
    row_t = lax.broadcasted_iota(jnp.int32, (tall, 2 * width), 0)
    half = EDGE // 2

    pick = row_r[:, :rows] == lane_r[:, :rows]

    def to_rows(ref):
        spread = jnp.broadcast_to(ref[...].astype(jnp.float32), (rows, rows))
        return jnp.sum(jnp.where(pick, spread, 0.0), axis=1, keepdims=True)

    shift = jnp.broadcast_to(to_rows(shift_ref).astype(jnp.int32), (rows, width))
    weight = jnp.broadcast_to(to_rows(frac_ref), (rows, width))

    load_f.wait()
    load_v.wait()

    for i in range(total // 2):
        a, b = xin[2 * i, rows - EDGE :, :], xin[2 * i + 1, rows - EDGE :, :]
        row_hi[i] = jnp.where(sub8 >= half, a, pltpu.roll(b, half, 0))
        a, b = xin[2 * i, :EDGE, :], xin[2 * i + 1, :EDGE, :]
        row_lo[i] = jnp.where(sub8 < half, a, pltpu.roll(b, half, 0))
    hi = xin[0]
    lo = xin[0]
    hi = pltpu.roll(hi, EDGE, 1)
    for j in range(1, total):
        x = xin[j]
        mine = (lane_r >= EDGE * j) & (lane_r < EDGE * (j + 1))
        hi = jnp.where(mine, pltpu.roll(x, (EDGE * (j + 1)) % width, 1), hi)
        lo = jnp.where(mine, pltpu.roll(x, EDGE * j, 1), lo)
    edge_hi[...] = hi
    edge_lo[...] = lo

    pl.semaphore_wait(
        barrier, 3 + 3 * has_dn.astype(jnp.int32) + 3 * has_up.astype(jnp.int32)
    )

    def remote(src, dst, k, a, r):
        return pltpu.make_async_remote_copy(
            src_ref=src, dst_ref=dst, send_sem=send_h.at[k], recv_sem=recv_h.at[k],
            device_id=dev(a, r), device_id_type=pl.DeviceIdType.MESH,
        )

    top = pl.ds(rows - EDGE, EDGE)
    bottom = pl.ds(0, EDGE)
    mid = pl.ds(EDGE, rows)
    after = pl.ds(EDGE + rows, EDGE)
    before = pl.ds(0, EDGE)
    to_up = [
        remote(row_hi, halo_d, 2, az, rad + 1),
        remote(edge_hi.at[top], halo_l.at[before], 3, right, rad + 1),
        remote(edge_lo.at[top], halo_r.at[before], 4, left, rad + 1),
    ]
    to_dn = [
        remote(row_lo, halo_u, 5, az, rad - 1),
        remote(edge_hi.at[bottom], halo_l.at[after], 6, right, rad - 1),
        remote(edge_lo.at[bottom], halo_r.at[after], 7, left, rad - 1),
    ]
    sides = [
        remote(edge_hi, halo_l.at[mid], 0, right, rad),
        remote(edge_lo, halo_r.at[mid], 1, left, rad),
    ]
    for c in sides:
        c.start()

    @pl.when(has_up)
    def _():
        for c in to_up:
            c.start()

    @pl.when(has_dn)
    def _():
        for c in to_dn:
            c.start()

    for c in sides:
        c.wait()

    @pl.when(has_dn)
    def _():
        for c in to_up:
            c.wait_recv()
        for c in to_dn:
            c.wait_send()

    @pl.when(has_up)
    def _():
        for c in to_dn:
            c.wait_recv()
        for c in to_up:
            c.wait_send()

    inside = jnp.logical_and(
        jnp.logical_or(row_t >= EDGE, has_dn),
        jnp.logical_or(row_t < EDGE + rows, has_up),
    )

    def extended(j, pair, odd):
        below, above = halo_d[pair], halo_u[pair]
        below = jnp.where(odd, pltpu.roll(below, half, 0), below)
        above = jnp.where(odd, pltpu.roll(above, half, 0), above)
        own = jnp.concatenate([below, xin[j], above], axis=0)
        r = pltpu.roll(halo_r[...], width - EDGE * j, 1)
        l = pltpu.roll(halo_l[...], 2 * width - EDGE * (j + 1), 1)
        ext = jnp.where(lane_t < width // 2, r, l)
        whole = jnp.concatenate([own, ext], axis=1)
        return jnp.where(inside, whole, 0.0)

    def prev(x, axis):
        return pltpu.roll(x, 1, axis)

    def nxt(x, axis):
        return pltpu.roll(x, x.shape[axis] - 1, axis)

    for layer in range(layers):
        jr, ja = slabs + layer, slabs + layers + layer
        vr = extended(jr, jr // 2, jr % 2 == 1)
        va = extended(ja, ja // 2, ja % 2 == 1)
        face_r = 0.5 * (prev(vr, 0) + vr)
        face_a = 0.5 * (prev(va, 1) + va)
        rp, rm = jnp.maximum(face_r, 0.0), jnp.minimum(face_r, 0.0)
        ap, am = jnp.maximum(face_a, 0.0), jnp.minimum(face_a, 0.0)
        mid_c = 1.0 + ((rm - nxt(rp, 0)) + (am - nxt(ap, 1)))
        coef[layer, 0] = jnp.where(inside, mid_c, 0.0)
        coef[layer, 1] = jnp.where(inside, rp, 0.0)
        coef[layer, 2] = jnp.where(inside, -nxt(rm, 0), 0.0)
        coef[layer, 3] = jnp.where(inside, ap, 0.0)
        coef[layer, 4] = jnp.where(inside, -nxt(am, 1), 0.0)

    source = (lane_r - shift) & (width - 1)

    def send_a_of(j):
        return pltpu.make_async_remote_copy(
            src_ref=rot.at[j], dst_ref=got.at[j], send_sem=send_a.at[j], recv_sem=recv_a.at[j],
            device_id=dev(right, rad), device_id_type=pl.DeviceIdType.MESH,
        )

    def send_b_of(j):
        return pltpu.make_async_remote_copy(
            src_ref=tail.at[j], dst_ref=got_tail.at[j], send_sem=send_b.at[j], recv_sem=recv_b.at[j],
            device_id=dev(right2, rad), device_id_type=pl.DeviceIdType.MESH,
        )

    quarter = width // 4
    rows4 = rows // 4

    def slab_of(i):
        return lax.rem(i, fields) * layers + lax.div(i, fields), lax.div(i, fields)

    def work(i, carry):
        j, layer = slab_of(i)
        v = extended(j, lax.div(j, layers), layer == 1)

        def stencil(x):
            return (
                coef[layer, 0] * x
                + coef[layer, 1] * prev(x, 0)
                + coef[layer, 2] * nxt(x, 0)
                + coef[layer, 3] * prev(x, 1)
                + coef[layer, 4] * nxt(x, 1)
            )

        for _ in range(STEPS):
            v = 0.5 * (v + stencil(stencil(v)))
        lead = v[EDGE : EDGE + rows, :width]
        trail = prev(v, 1)[EDGE : EDGE + rows, :width]
        y = (1.0 - weight) * lead + weight * trail
        turned = jnp.take_along_axis(y, source, axis=1, mode="promise_in_bounds")
        rot[j] = turned
        send_a_of(j).start()
        packed = turned[:rows4]
        lane_q = lane_r[:rows4]
        for q in range(1, 4):
            part = pltpu.roll(turned[q * rows4 : (q + 1) * rows4], q * quarter, 1)
            packed = jnp.where(lane_q >= q * quarter, part, packed)
        tail[j] = packed
        send_b_of(j).start()
        return carry

    lax.fori_loop(0, slabs, work, 0)

    def out_of(j):
        return pltpu.make_async_copy(done.at[j], out.at[j], out_sem.at[j])

    def finish(i, carry):
        j, _ = slab_of(i)
        send_a_of(j).wait_recv()
        send_b_of(j).wait_recv()
        b = got_tail[j]
        parts = [b] + [pltpu.roll(b, width - q * quarter, 1) for q in range(1, 4)]
        far = jnp.concatenate(parts, axis=0)
        near = jnp.where(lane_r >= shift - width, got[j], far)
        done[j] = jnp.where(lane_r >= shift, rot[j], near)
        out_of(j).start()
        return carry

    lax.fori_loop(0, slabs, finish, 0)

    def drain(i, carry):
        j, _ = slab_of(i)
        send_a_of(j).wait_send()
        send_b_of(j).wait_send()
        out_of(j).wait()
        return carry

    lax.fori_loop(0, slabs, drain, 0)


def on_device(fluid_state, velocity, shifts, fraction):
    fields, layers, rows, width = fluid_state.shape
    n_az, n_rad = lax.axis_size("az"), lax.axis_size("rad")
    slabs, vels = fields * layers, 2 * layers
    total = slabs + vels
    tall = rows + 2 * EDGE
    f32 = jnp.float32
    dma = pltpu.SemaphoreType.DMA
    anywhere = pl.BlockSpec(memory_space=pl.ANY)
    vmem = pl.BlockSpec(memory_space=pltpu.VMEM)
    result = pl.pallas_call(
        functools.partial(kernel, n_az, n_rad, fields, layers),
        out_shape=jax.ShapeDtypeStruct((slabs, rows, width), f32),
        in_specs=[anywhere, anywhere, vmem, vmem],
        out_specs=anywhere,
        scratch_shapes=[
            pltpu.VMEM((total, rows, width), f32),
            pltpu.VMEM((rows, width), f32),
            pltpu.VMEM((rows, width), f32),
            pltpu.VMEM((total // 2, EDGE, width), f32),
            pltpu.VMEM((total // 2, EDGE, width), f32),
            pltpu.VMEM((tall, width), f32),
            pltpu.VMEM((tall, width), f32),
            pltpu.VMEM((total // 2, EDGE, width), f32),
            pltpu.VMEM((total // 2, EDGE, width), f32),
            pltpu.VMEM((layers, 5, tall, 2 * width), f32),
            pltpu.VMEM((slabs, rows, width), f32),
            pltpu.VMEM((slabs, rows // 4, width), f32),
            pltpu.VMEM((slabs, rows, width), f32),
            pltpu.VMEM((slabs, rows // 4, width), f32),
            pltpu.VMEM((slabs, rows, width), f32),
            dma((2,)), dma((8,)), dma((8,)),
            dma((slabs,)), dma((slabs,)), dma((slabs,)), dma((slabs,)), dma((slabs,)),
        ],
        compiler_params=pltpu.CompilerParams(
            collective_id=0, has_side_effects=True, vmem_limit_bytes=16 * 1024 * 1024
        ),
        cost_estimate=pl.CostEstimate(
            flops=50_000_000, bytes_accessed=800_000, transcendentals=0
        ),
    )(
        fluid_state.reshape(slabs, rows, width),
        velocity.reshape(vels, rows, width),
        shifts.reshape(1, rows),
        fraction.reshape(1, rows),
    )
    return result.reshape(fields, layers, rows, width)


def solution(mesh):
    return jax.shard_map(
        on_device,
        mesh=mesh,
        in_specs=(P(None, None, "rad", "az"), P(None, None, "rad", "az"), P("rad"), P("rad")),
        out_specs=P(None, None, "rad", "az"),
        check_vma=False,
    )
```

```python
import functools

import jax
import jax.numpy as jnp
from jax import lax
from jax.experimental import pallas as pl
from jax.experimental.pallas import tpu as pltpu
from jax.sharding import PartitionSpec as P

STEPS = 2
EDGE = 8
NINE = 9


def kernel(
    n_az, n_rad, fields, layers,
    fluid, vel, shift_hbm, frac_hbm, out,
    shift_ref, frac_ref, shift_b, weight_b, xin, own_lo, own_hi, row_lo, row_hi, halo_l, halo_r, halo_d, halo_u,
    coef, coef_s, coef_t, inner, rot, tail, got, got_tail,
    in_sem, send_h, recv_h, send_a, recv_a, send_b, recv_b,
):
    slabs = fields * layers
    vels = 2 * layers
    total = slabs + vels
    rows, width = xin.shape[1], xin.shape[2]
    tall = rows + 2 * EDGE
    az = lax.axis_index("az")
    rad = lax.axis_index("rad")
    right = lax.rem(az + 1, n_az)
    right2 = lax.rem(az + 2, n_az)
    left = lax.rem(az + n_az - 1, n_az)
    left2 = lax.rem(az + n_az - 2, n_az)
    has_dn = rad > 0
    has_up = rad < n_rad - 1

    def dev(a, r):
        return {"az": a, "rad": r}

    load_f = pltpu.make_async_copy(fluid, xin.at[pl.ds(0, slabs)], in_sem.at[0])
    load_v = pltpu.make_async_copy(vel, xin.at[pl.ds(slabs, vels)], in_sem.at[1])
    load_s = pltpu.make_async_copy(shift_hbm, shift_ref, in_sem.at[2])
    load_w = pltpu.make_async_copy(frac_hbm, frac_ref, in_sem.at[3])
    loads = (load_s, load_w, load_f, load_v)
    for c in loads:
        c.start()

    barrier = pltpu.get_barrier_semaphore()
    for a in (left, right, left2):
        pl.semaphore_signal(barrier, inc=1, device_id=dev(a, rad))

    @pl.when(has_dn)
    def _():
        for a in (left, az, right):
            pl.semaphore_signal(barrier, inc=1, device_id=dev(a, rad - 1))

    @pl.when(has_up)
    def _():
        for a in (left, az, right):
            pl.semaphore_signal(barrier, inc=1, device_id=dev(a, rad + 1))

    def iota(shape, axis):
        return lax.broadcasted_iota(jnp.int32, shape, axis)

    sub8 = iota((EDGE, width), 0)
    lane_r = iota((rows, width), 1)
    half = EDGE // 2
    own = pl.ds(EDGE, rows)

    for c in loads:
        c.wait()

    for i in range(total // 2):
        a, b = xin[2 * i, rows - EDGE :, :], xin[2 * i + 1, rows - EDGE :, :]
        row_hi[i] = jnp.where(sub8 >= half, a, pltpu.roll(b, half, 0))
        a, b = xin[2 * i, :EDGE, :], xin[2 * i + 1, :EDGE, :]
        row_lo[i] = jnp.where(sub8 < half, a, pltpu.roll(b, half, 0))
    lo = xin[0]
    hi = pltpu.roll(xin[0], NINE, 1)
    for j in range(1, total):
        x = xin[j]
        mine = lane_r >= NINE * j
        hi = jnp.where(mine, pltpu.roll(x, (NINE * (j + 1)) % width, 1), hi)
        lo = jnp.where(mine, pltpu.roll(x, NINE * j, 1), lo)
    own_hi[own, :] = hi
    own_lo[own, :] = lo

    def prev(x, axis):
        return pltpu.roll(x, 1, axis)

    def nxt(x, axis):
        return pltpu.roll(x, x.shape[axis] - 1, axis)

    def coefficients(vr, va, keep):
        face_r = 0.5 * (prev(vr, 0) + vr)
        face_a = 0.5 * (prev(va, 1) + va)
        rp, rm = jnp.maximum(face_r, 0.0), jnp.minimum(face_r, 0.0)
        ap, am = jnp.maximum(face_a, 0.0), jnp.minimum(face_a, 0.0)
        mid_c = 1.0 + ((rm - nxt(rp, 0)) + (am - nxt(ap, 1)))
        all5 = [mid_c, rp, -nxt(rm, 0), ap, -nxt(am, 1)]
        if keep is not None:
            all5 = [jnp.where(keep, c, 0.0) for c in all5]
        return all5

    def transport(values, pick):
        def stencil(n, x):
            return (
                (pick(n, 0) * x + pick(n, 1) * prev(x, 0))
                + (pick(n, 2) * nxt(x, 0) + pick(n, 3) * prev(x, 1))
                + pick(n, 4) * nxt(x, 1)
            )

        for _ in range(STEPS):
            once = [stencil(n, x) for n, x in enumerate(values)]
            twice = [stencil(n, x) for n, x in enumerate(once)]
            values = [0.5 * (x + t) for x, t in zip(values, twice)]
        return values

    for layer in range(layers):
        cs = coefficients(xin[slabs + layer], xin[slabs + layers + layer], None)
        for k in range(5):
            coef[layer, k] = cs[k]

    pick_row = iota((rows, rows), 0) == iota((rows, rows), 1)

    def to_rows(ref):
        spread = jnp.broadcast_to(ref[...].astype(jnp.float32), (rows, rows))
        return jnp.sum(jnp.where(pick_row, spread, 0.0), axis=1, keepdims=True)

    shift_b[...] = jnp.broadcast_to(to_rows(shift_ref).astype(jnp.int32), (rows, width))
    weight_b[...] = jnp.broadcast_to(to_rows(frac_ref), (rows, width))

    pl.semaphore_wait(
        barrier, 3 + 3 * has_dn.astype(jnp.int32) + 3 * has_up.astype(jnp.int32)
    )

    def remote(src, dst, k, a, r):
        return pltpu.make_async_remote_copy(
            src_ref=src, dst_ref=dst, send_sem=send_h.at[k], recv_sem=recv_h.at[k],
            device_id=dev(a, r), device_id_type=pl.DeviceIdType.MESH,
        )

    top = pl.ds(rows, EDGE)
    bottom = pl.ds(EDGE, EDGE)
    after = pl.ds(EDGE + rows, EDGE)
    before = pl.ds(0, EDGE)
    to_up = [
        remote(own_hi.at[top], halo_l.at[before], 3, right, rad + 1),
        remote(own_lo.at[top], halo_r.at[before], 4, left, rad + 1),
        remote(own_hi.at[top], own_hi.at[before], 8, az, rad + 1),
        remote(own_lo.at[top], own_lo.at[before], 9, az, rad + 1),
        remote(row_hi, halo_d, 2, az, rad + 1),
    ]
    to_dn = [
        remote(own_hi.at[bottom], halo_l.at[after], 6, right, rad - 1),
        remote(own_lo.at[bottom], halo_r.at[after], 7, left, rad - 1),
        remote(own_hi.at[bottom], own_hi.at[after], 10, az, rad - 1),
        remote(own_lo.at[bottom], own_lo.at[after], 11, az, rad - 1),
        remote(row_lo, halo_u, 5, az, rad - 1),
    ]
    sides = [
        remote(own_hi.at[own], halo_l.at[own], 0, right, rad),
        remote(own_lo.at[own], halo_r.at[own], 1, left, rad),
    ]
    for c in sides:
        c.start()

    @pl.when(has_up)
    def _():
        for c in to_up:
            c.start()

    @pl.when(has_dn)
    def _():
        for c in to_dn:
            c.start()

    def interior(layer, carry):
        values = [xin[f * layers + layer] for f in range(fields)]
        values = transport(values, lambda n, k: coef[layer, k])
        weight = weight_b[...]
        for f, v in enumerate(values):
            inner[f * layers + layer] = (1.0 - weight) * v + weight * prev(v, 1)
        return carry

    lax.fori_loop(0, layers, interior, 0)

    for c in sides:
        c.wait()

    @pl.when(has_dn)
    def _():
        for c in to_up:
            c.wait_recv()
        for c in to_dn:
            c.wait_send()

    @pl.when(has_up)
    def _():
        for c in to_dn:
            c.wait_recv()
        for c in to_up:
            c.wait_send()

    weight, shift = weight_b[...], shift_b[...]

    row_s = iota((4 * EDGE, width), 0)
    keep_s = jnp.logical_and(
        jnp.logical_or(row_s >= EDGE, has_dn), jnp.logical_or(row_s < 3 * EDGE, has_up)
    )

    def strip(j):
        below, above = halo_d[j // 2], halo_u[j // 2]
        if j % 2:
            below, above = pltpu.roll(below, half, 0), pltpu.roll(above, half, 0)
        both = jnp.concatenate([below, xin[j, :EDGE], xin[j, rows - EDGE :], above], axis=0)
        return jnp.where(keep_s, both, 0.0)

    for layer in range(layers):
        cs = coefficients(strip(slabs + layer), strip(slabs + layers + layer), keep_s)
        for k in range(5):
            coef_s[layer, k] = cs[k]

    lane_t = iota((tall, width), 1)
    row_t = iota((tall, width), 0)
    keep_t = jnp.logical_and(
        jnp.logical_or(row_t >= EDGE, has_dn), jnp.logical_or(row_t < EDGE + rows, has_up)
    )
    k16 = lane_t & 15
    group = lane_t >> 4
    on_right = (group & 1) == 1
    layer_of = (group >> 1) & 1
    part_of = group >> 2
    lag = NINE - 7
    offset = jnp.where(
        on_right,
        jnp.where(k16 < NINE, k16, k16 - NINE),
        jnp.where(k16 < 7, k16 + lag, k16 - 7),
    )
    use_l = jnp.logical_and(jnp.logical_not(on_right), k16 < 7)
    use_r = jnp.logical_and(on_right, k16 >= NINE)

    def take(x, index):
        return jnp.take_along_axis(x, index, axis=1, mode="promise_in_bounds")

    def columns(slab):
        index = NINE * slab + offset
        mine = jnp.where(on_right, take(own_hi[...], index), take(own_lo[...], index))
        x = jnp.where(use_l, take(halo_l[...], index), mine)
        x = jnp.where(use_r, take(halo_r[...], index), x)
        return jnp.where(keep_t, x, 0.0)

    cs = coefficients(
        columns(slabs + layer_of), columns(slabs + layers + layer_of), keep_t
    )
    for k in range(5):
        coef_t[k] = cs[k]

    tiles = (fields + 1) // 2
    cols = [
        columns(jnp.minimum(2 * t + part_of, fields - 1) * layers + layer_of)
        for t in range(tiles)
    ]
    cols = transport(cols, lambda n, k: coef_t[k])
    cols_y = []
    for v in cols:
        v, p = v[EDGE : EDGE + rows], prev(v, 1)[EDGE : EDGE + rows]
        cols_y.append((1.0 - weight) * v + weight * p)

    for layer in range(layers):
        js = [f * layers + layer for f in range(fields)]
        values = transport([strip(j) for j in js], lambda n, k: coef_s[layer, k])
        for j, v in zip(js, values):
            p = prev(v, 1)
            for lo_row, at, first in ((EDGE, 0, True), (2 * EDGE, rows - EDGE, False)):
                w = weight[at : at + EDGE]
                y = (1.0 - w) * v[lo_row : lo_row + EDGE] + w * p[lo_row : lo_row + EDGE]
                keep = sub8 < half if first else sub8 >= half
                inner[j, at : at + EDGE, :] = jnp.where(keep, y, inner[j, at : at + EDGE, :])

    source = (lane_r - shift) & (width - 1)
    in_strip = jnp.logical_or(source <= 4, source >= width - 4)
    strip_lane = jnp.where(source < width // 2, source + 7, source - (width - NINE) + 16)

    def send_a_of(j):
        return pltpu.make_async_remote_copy(
            src_ref=rot.at[j], dst_ref=got.at[j], send_sem=send_a.at[j], recv_sem=recv_a.at[j],
            device_id=dev(right, rad), device_id_type=pl.DeviceIdType.MESH,
        )

    def send_b_of(j):
        return pltpu.make_async_remote_copy(
            src_ref=tail.at[j], dst_ref=got_tail.at[j], send_sem=send_b.at[j], recv_sem=recv_b.at[j],
            device_id=dev(right2, rad), device_id_type=pl.DeviceIdType.MESH,
        )

    quarter = width // 4
    rows4 = rows // 4

    lane_q = lane_r[:rows4]
    for f in range(fields):
        for layer in range(layers):
            j = f * layers + layer
            at = (strip_lane + (64 * (f % 2) + 32 * layer)) & (width - 1)
            turned = jnp.where(in_strip, take(cols_y[f // 2], at), take(inner[j], source))
            rot[j] = turned
            send_a_of(j).start()
            packed = turned[:rows4]
            for q in range(1, 4):
                part = pltpu.roll(turned[q * rows4 : (q + 1) * rows4], q * quarter, 1)
                packed = jnp.where(lane_q >= q * quarter, part, packed)
            tail[j] = packed
            send_b_of(j).start()

    def finish(j, carry):
        send_a_of(j).wait_recv()
        send_b_of(j).wait_recv()
        b = got_tail[j]
        parts = [b] + [pltpu.roll(b, width - q * quarter, 1) for q in range(1, 4)]
        far = jnp.concatenate(parts, axis=0)
        near = jnp.where(lane_r >= shift - width, got[j], far)
        out[j] = jnp.where(lane_r >= shift, rot[j], near)
        return carry

    lax.fori_loop(0, slabs, finish, 0)

    def drain(j, carry):
        send_a_of(j).wait_send()
        send_b_of(j).wait_send()
        return carry

    lax.fori_loop(0, slabs, drain, 0)


def on_device(fluid_state, velocity, shifts, fraction):
    fields, layers, rows, width = fluid_state.shape
    n_az, n_rad = lax.axis_size("az"), lax.axis_size("rad")
    slabs, vels = fields * layers, 2 * layers
    total = slabs + vels
    tall = rows + 2 * EDGE
    f32 = jnp.float32
    dma = pltpu.SemaphoreType.DMA
    hbm = pl.BlockSpec(memory_space=pltpu.HBM)
    vmem = pl.BlockSpec(memory_space=pltpu.VMEM)
    result = pl.pallas_call(
        functools.partial(kernel, n_az, n_rad, fields, layers),
        out_shape=jax.ShapeDtypeStruct((slabs, rows, width), f32),
        in_specs=[hbm, hbm, hbm, hbm],
        out_specs=vmem,
        scratch_shapes=[
            pltpu.VMEM((1, rows), jnp.int32),
            pltpu.VMEM((1, rows), f32),
            pltpu.VMEM((rows, width), jnp.int32),
            pltpu.VMEM((rows, width), f32),
            pltpu.VMEM((total, rows, width), f32),
            pltpu.VMEM((tall, width), f32),
            pltpu.VMEM((tall, width), f32),
            pltpu.VMEM((total // 2, EDGE, width), f32),
            pltpu.VMEM((total // 2, EDGE, width), f32),
            pltpu.VMEM((tall, width), f32),
            pltpu.VMEM((tall, width), f32),
            pltpu.VMEM((total // 2, EDGE, width), f32),
            pltpu.VMEM((total // 2, EDGE, width), f32),
            pltpu.VMEM((layers, 5, rows, width), f32),
            pltpu.VMEM((layers, 5, 4 * EDGE, width), f32),
            pltpu.VMEM((5, tall, width), f32),
            pltpu.VMEM((slabs, rows, width), f32),
            pltpu.VMEM((slabs, rows, width), f32),
            pltpu.VMEM((slabs, rows // 4, width), f32),
            pltpu.VMEM((slabs, rows, width), f32),
            pltpu.VMEM((slabs, rows // 4, width), f32),
            dma((4,)), dma((12,)), dma((12,)),
            dma((slabs,)), dma((slabs,)), dma((slabs,)), dma((slabs,)),
        ],
        compiler_params=pltpu.CompilerParams(
            collective_id=0, has_side_effects=True, vmem_limit_bytes=60 * 1024 * 1024
        ),
        cost_estimate=pl.CostEstimate(
            flops=50_000_000, bytes_accessed=800_000, transcendentals=0
        ),
    )(
        fluid_state.reshape(slabs, rows, width),
        velocity.reshape(vels, rows, width),
        shifts.reshape(1, rows),
        fraction.reshape(1, rows),
    )
    return result.reshape(fields, layers, rows, width)


def solution(mesh):
    return jax.shard_map(
        on_device,
        mesh=mesh,
        in_specs=(P(None, None, "rad", "az"), P(None, None, "rad", "az"), P("rad"), P("rad")),
        out_specs=P(None, None, "rad", "az"),
        check_vma=False,
    )
```

```python
import functools

import jax
import jax.numpy as jnp
from jax import lax
from jax.experimental import pallas as pl
from jax.experimental.pallas import tpu as pltpu
from jax.sharding import PartitionSpec as P

STEPS = 2
EDGE = 8
NINE = 9


def kernel(
    n_az, n_rad, fields, layers,
    fluid, vel, shift_hbm, frac_hbm, out,
    shift_ref, frac_ref, shift_b, weight_b, xin, own_lo, own_hi, row_lo, row_hi, halo_l, halo_r, halo_d, halo_u,
    coef, coef_s, coef_t, seam, brim, got_brim, brim_tail, got_brim_tail, rot, tail, got, got_tail,
    in_sem, send_h, recv_h, send_a, recv_a, send_b, recv_b,
):
    slabs = fields * layers
    vels = 2 * layers
    total = slabs + vels
    rows, width = xin.shape[1], xin.shape[2]
    tall = rows + 2 * EDGE
    az = lax.axis_index("az")
    rad = lax.axis_index("rad")
    right = lax.rem(az + 1, n_az)
    right2 = lax.rem(az + 2, n_az)
    left = lax.rem(az + n_az - 1, n_az)
    left2 = lax.rem(az + n_az - 2, n_az)
    has_dn = rad > 0
    has_up = rad < n_rad - 1

    def dev(a, r):
        return {"az": a, "rad": r}

    load_f = pltpu.make_async_copy(fluid, xin.at[pl.ds(0, slabs)], in_sem.at[0])
    load_v = pltpu.make_async_copy(vel, xin.at[pl.ds(slabs, vels)], in_sem.at[1])
    load_s = pltpu.make_async_copy(shift_hbm, shift_ref, in_sem.at[2])
    load_w = pltpu.make_async_copy(frac_hbm, frac_ref, in_sem.at[3])
    loads = (load_s, load_w, load_f, load_v)
    for c in loads:
        c.start()

    barrier = pltpu.get_barrier_semaphore()
    for a in (left, right, left2):
        pl.semaphore_signal(barrier, inc=1, device_id=dev(a, rad))

    @pl.when(has_dn)
    def _():
        for a in (left, az, right):
            pl.semaphore_signal(barrier, inc=1, device_id=dev(a, rad - 1))

    @pl.when(has_up)
    def _():
        for a in (left, az, right):
            pl.semaphore_signal(barrier, inc=1, device_id=dev(a, rad + 1))

    quarter = width // 4
    rows4 = rows // 4

    def iota(shape, axis):
        return lax.broadcasted_iota(jnp.int32, shape, axis)

    sub8 = iota((EDGE, width), 0)
    lane_r = iota((rows, width), 1)
    half = EDGE // 2
    own = pl.ds(EDGE, rows)

    for c in loads:
        c.wait()

    for i in range(total // 2):
        a, b = xin[2 * i, rows - EDGE :, :], xin[2 * i + 1, rows - EDGE :, :]
        row_hi[i] = jnp.where(sub8 >= half, a, pltpu.roll(b, half, 0))
        a, b = xin[2 * i, :EDGE, :], xin[2 * i + 1, :EDGE, :]
        row_lo[i] = jnp.where(sub8 < half, a, pltpu.roll(b, half, 0))
    lo = xin[0]
    hi = pltpu.roll(xin[0], NINE, 1)
    for j in range(1, total):
        x = xin[j]
        mine = lane_r >= NINE * j
        hi = jnp.where(mine, pltpu.roll(x, (NINE * (j + 1)) % width, 1), hi)
        lo = jnp.where(mine, pltpu.roll(x, NINE * j, 1), lo)
    own_hi[own, :] = hi
    own_lo[own, :] = lo

    def prev(x, axis):
        return pltpu.roll(x, 1, axis)

    def nxt(x, axis):
        return pltpu.roll(x, x.shape[axis] - 1, axis)

    def coefficients(vr, va, keep):
        face_r = 0.5 * (prev(vr, 0) + vr)
        face_a = 0.5 * (prev(va, 1) + va)
        rp, rm = jnp.maximum(face_r, 0.0), jnp.minimum(face_r, 0.0)
        ap, am = jnp.maximum(face_a, 0.0), jnp.minimum(face_a, 0.0)
        mid_c = 1.0 + ((rm - nxt(rp, 0)) + (am - nxt(ap, 1)))
        all5 = [mid_c, rp, -nxt(rm, 0), ap, -nxt(am, 1)]
        if keep is not None:
            all5 = [jnp.where(keep, c, 0.0) for c in all5]
        return all5

    def transport(values, pick):
        def stencil(n, x):
            return (
                (pick(n, 0) * x + pick(n, 1) * prev(x, 0))
                + (pick(n, 2) * nxt(x, 0) + pick(n, 3) * prev(x, 1))
                + pick(n, 4) * nxt(x, 1)
            )

        for _ in range(STEPS):
            once = [stencil(n, x) for n, x in enumerate(values)]
            twice = [stencil(n, x) for n, x in enumerate(once)]
            values = [0.5 * (x + t) for x, t in zip(values, twice)]
        return values

    for layer in range(layers):
        cs = coefficients(xin[slabs + layer], xin[slabs + layers + layer], None)
        for k in range(5):
            coef[layer, k] = cs[k]

    pick_row = iota((rows, rows), 0) == iota((rows, rows), 1)

    def to_rows(ref):
        spread = jnp.broadcast_to(ref[...].astype(jnp.float32), (rows, rows))
        return jnp.sum(jnp.where(pick_row, spread, 0.0), axis=1, keepdims=True)

    shift_b[...] = jnp.broadcast_to(to_rows(shift_ref).astype(jnp.int32), (rows, width))
    weight_b[...] = jnp.broadcast_to(to_rows(frac_ref), (rows, width))

    pl.semaphore_wait(
        barrier, 3 + 3 * has_dn.astype(jnp.int32) + 3 * has_up.astype(jnp.int32)
    )

    def remote(src, dst, k, a, r):
        return pltpu.make_async_remote_copy(
            src_ref=src, dst_ref=dst, send_sem=send_h.at[k], recv_sem=recv_h.at[k],
            device_id=dev(a, r), device_id_type=pl.DeviceIdType.MESH,
        )

    top = pl.ds(rows, EDGE)
    bottom = pl.ds(EDGE, EDGE)
    after = pl.ds(EDGE + rows, EDGE)
    before = pl.ds(0, EDGE)
    to_up = [
        remote(own_hi.at[top], halo_l.at[before], 3, right, rad + 1),
        remote(own_lo.at[top], halo_r.at[before], 4, left, rad + 1),
        remote(own_hi.at[top], own_hi.at[before], 8, az, rad + 1),
        remote(own_lo.at[top], own_lo.at[before], 9, az, rad + 1),
        remote(row_hi, halo_d, 2, az, rad + 1),
    ]
    to_dn = [
        remote(own_hi.at[bottom], halo_l.at[after], 6, right, rad - 1),
        remote(own_lo.at[bottom], halo_r.at[after], 7, left, rad - 1),
        remote(own_hi.at[bottom], own_hi.at[after], 10, az, rad - 1),
        remote(own_lo.at[bottom], own_lo.at[after], 11, az, rad - 1),
        remote(row_lo, halo_u, 5, az, rad - 1),
    ]
    sides = [
        remote(own_hi.at[own], halo_l.at[own], 0, right, rad),
        remote(own_lo.at[own], halo_r.at[own], 1, left, rad),
    ]
    for c in sides:
        c.start()

    @pl.when(has_up)
    def _():
        for c in to_up:
            c.start()

    @pl.when(has_dn)
    def _():
        for c in to_dn:
            c.start()

    def send_a_of(j):
        return pltpu.make_async_remote_copy(
            src_ref=rot.at[j], dst_ref=got.at[j], send_sem=send_a.at[j], recv_sem=recv_a.at[j],
            device_id=dev(right, rad), device_id_type=pl.DeviceIdType.MESH,
        )

    def send_b_of(j):
        return pltpu.make_async_remote_copy(
            src_ref=tail.at[j], dst_ref=got_tail.at[j], send_sem=send_b.at[j], recv_sem=recv_b.at[j],
            device_id=dev(right2, rad), device_id_type=pl.DeviceIdType.MESH,
        )


    def take(x, index):
        return jnp.take_along_axis(x, index, axis=1, mode="promise_in_bounds")

    weight, shift = weight_b[...], shift_b[...]
    source = (lane_r - shift) & (width - 1)
    lane_q = lane_r[:rows4]

    def interior(layer, carry):
        values = [xin[f * layers + layer] for f in range(fields)]
        values = transport(values, lambda n, k: coef[layer, k])
        for f, v in enumerate(values):
            j = f * layers + layer
            y = (1.0 - weight) * v + weight * prev(v, 1)
            turned = take(y, source)
            rot[j] = turned
            send_a_of(j).start()
            packed = turned[:rows4]
            for q in range(1, 4):
                part = pltpu.roll(turned[q * rows4 : (q + 1) * rows4], q * quarter, 1)
                packed = jnp.where(lane_q >= q * quarter, part, packed)
            tail[j] = packed
            send_b_of(j).start()
        return carry

    lax.fori_loop(0, layers, interior, 0)

    for c in sides:
        c.wait()

    @pl.when(has_dn)
    def _():
        for c in to_up:
            c.wait_recv()
        for c in to_dn:
            c.wait_send()

    @pl.when(has_up)
    def _():
        for c in to_dn:
            c.wait_recv()
        for c in to_up:
            c.wait_send()

    row_s = iota((4 * EDGE, width), 0)
    keep_s = jnp.logical_and(
        jnp.logical_or(row_s >= EDGE, has_dn), jnp.logical_or(row_s < 3 * EDGE, has_up)
    )

    def strip(j):
        below, above = halo_d[j // 2], halo_u[j // 2]
        if j % 2:
            below, above = pltpu.roll(below, half, 0), pltpu.roll(above, half, 0)
        both = jnp.concatenate([below, xin[j, :EDGE], xin[j, rows - EDGE :], above], axis=0)
        return jnp.where(keep_s, both, 0.0)

    for layer in range(layers):
        cs = coefficients(strip(slabs + layer), strip(slabs + layers + layer), keep_s)
        for k in range(5):
            coef_s[layer, k] = cs[k]

    lane_t = iota((tall, width), 1)
    row_t = iota((tall, width), 0)
    keep_t = jnp.logical_and(
        jnp.logical_or(row_t >= EDGE, has_dn), jnp.logical_or(row_t < EDGE + rows, has_up)
    )
    k16 = lane_t & 15
    group = lane_t >> 4
    on_right = (group & 1) == 1
    layer_of = (group >> 1) & 1
    part_of = group >> 2
    lag = NINE - 7
    offset = jnp.where(
        on_right,
        jnp.where(k16 < NINE, k16, k16 - NINE),
        jnp.where(k16 < 7, k16 + lag, k16 - 7),
    )
    use_l = jnp.logical_and(jnp.logical_not(on_right), k16 < 7)
    use_r = jnp.logical_and(on_right, k16 >= NINE)

    def columns(slab):
        index = NINE * slab + offset
        mine = jnp.where(on_right, take(own_hi[...], index), take(own_lo[...], index))
        x = jnp.where(use_l, take(halo_l[...], index), mine)
        x = jnp.where(use_r, take(halo_r[...], index), x)
        return jnp.where(keep_t, x, 0.0)

    cs = coefficients(
        columns(slabs + layer_of), columns(slabs + layers + layer_of), keep_t
    )
    for k in range(5):
        coef_t[k] = cs[k]

    tiles = (fields + 1) // 2
    cols = [
        columns(jnp.minimum(2 * t + part_of, fields - 1) * layers + layer_of)
        for t in range(tiles)
    ]
    cols = transport(cols, lambda n, k: coef_t[k])
    cols_y = []
    for v in cols:
        v, p = v[EDGE : EDGE + rows], prev(v, 1)[EDGE : EDGE + rows]
        cols_y.append((1.0 - weight) * v + weight * p)

    slab_l = (lane_r * 57) >> 9
    m9 = lane_r - NINE * slab_l
    field_l, layer_l = slab_l // layers, slab_l % layers
    at = 64 * (field_l & 1) + 32 * layer_l + jnp.where(m9 < 5, m9 + 7, m9 + 16)
    at = at & (width - 1)
    s_tile = take(cols_y[tiles - 1], at)
    for t in range(tiles - 2, -1, -1):
        s_tile = jnp.where(field_l < 2 * (t + 1), take(cols_y[t], at), s_tile)
    seam[0] = s_tile

    first = sub8 < half

    def outer(x):
        return jnp.where(first, x[:EDGE], x[rows - EDGE :])

    w8, source8, lane8 = outer(weight), outer(source), iota((EDGE, width), 1)
    shift8 = outer(shift)
    spare = [None] * slabs
    for layer in range(layers):
        js = [f * layers + layer for f in range(fields)]
        values = transport([strip(j) for j in js], lambda n, k: coef_s[layer, k])
        for j, v in zip(js, values):
            p = prev(v, 1)
            v8 = jnp.where(first, v[EDGE : 2 * EDGE], v[2 * EDGE : 3 * EDGE])
            p8 = jnp.where(first, p[EDGE : 2 * EDGE], p[2 * EDGE : 3 * EDGE])
            spare[j] = take((1.0 - w8) * v8 + w8 * p8, source8)
            brim[j] = spare[j]
    groups = (slabs + 3) // 4
    for u in range(groups):
        packed = spare[4 * u]
        for q in range(1, min(4, slabs - 4 * u)):
            packed = jnp.where(
                lane8 >= q * quarter, pltpu.roll(spare[4 * u + q], q * quarter, 1), packed
            )
        brim_tail[u] = packed

    late = [
        remote(seam.at[0], seam.at[1], 12, right, rad),
        remote(brim, got_brim, 13, right, rad),
        remote(seam.at[0], seam.at[2], 14, right2, rad),
        remote(brim_tail, got_brim_tail, 15, right2, rad),
    ]
    for c in late:
        c.start()

    in_strip = jnp.logical_or(source <= 4, source >= width - 4)
    seam_lane = jnp.where(source <= 4, source, source - (width - NINE))
    here, next_ = lane_r >= shift, lane_r >= shift - width
    here8, next8 = lane8 >= shift8, lane8 >= shift8 - width

    def gather(j, carry):
        send_a_of(j).wait_recv()
        send_b_of(j).wait_recv()
        b = got_tail[j]
        parts = [b] + [pltpu.roll(b, width - q * quarter, 1) for q in range(1, 4)]
        far = jnp.concatenate(parts, axis=0)
        out[j] = jnp.where(here, rot[j], jnp.where(next_, got[j], far))
        return carry

    lax.fori_loop(0, slabs, gather, 0)
    for c in late:
        c.wait_recv()

    for j in range(slabs):
        at = (NINE * j + seam_lane) & (width - 1)
        patch = jnp.where(
            here, take(seam[0], at), jnp.where(next_, take(seam[1], at), take(seam[2], at))
        )
        q = j % 4
        far8 = got_brim_tail[j // 4]
        if q:
            far8 = pltpu.roll(far8, width - q * quarter, 1)
        rim = jnp.where(here8, brim[j], jnp.where(next8, got_brim[j], far8))
        base = jnp.concatenate(
            [
                jnp.where(first, rim, out[j, :EDGE]),
                out[j, EDGE : rows - EDGE],
                jnp.where(first, out[j, rows - EDGE :], rim),
            ],
            axis=0,
        )
        out[j] = jnp.where(in_strip, patch, base)

    for c in late:
        c.wait_send()

    def drain(j, carry):
        send_a_of(j).wait_send()
        send_b_of(j).wait_send()
        return carry

    lax.fori_loop(0, slabs, drain, 0)


def on_device(fluid_state, velocity, shifts, fraction):
    fields, layers, rows, width = fluid_state.shape
    n_az, n_rad = lax.axis_size("az"), lax.axis_size("rad")
    slabs, vels = fields * layers, 2 * layers
    total = slabs + vels
    tall = rows + 2 * EDGE
    f32 = jnp.float32
    dma = pltpu.SemaphoreType.DMA
    hbm = pl.BlockSpec(memory_space=pltpu.HBM)
    vmem = pl.BlockSpec(memory_space=pltpu.VMEM)
    result = pl.pallas_call(
        functools.partial(kernel, n_az, n_rad, fields, layers),
        out_shape=pltpu.VMEM((slabs, rows, width), f32),
        in_specs=[hbm, hbm, hbm, hbm],
        out_specs=vmem,
        scratch_shapes=[
            pltpu.VMEM((1, rows), jnp.int32),
            pltpu.VMEM((1, rows), f32),
            pltpu.VMEM((rows, width), jnp.int32),
            pltpu.VMEM((rows, width), f32),
            pltpu.VMEM((total, rows, width), f32),
            pltpu.VMEM((tall, width), f32),
            pltpu.VMEM((tall, width), f32),
            pltpu.VMEM((total // 2, EDGE, width), f32),
            pltpu.VMEM((total // 2, EDGE, width), f32),
            pltpu.VMEM((tall, width), f32),
            pltpu.VMEM((tall, width), f32),
            pltpu.VMEM((total // 2, EDGE, width), f32),
            pltpu.VMEM((total // 2, EDGE, width), f32),
            pltpu.VMEM((layers, 5, rows, width), f32),
            pltpu.VMEM((layers, 5, 4 * EDGE, width), f32),
            pltpu.VMEM((5, tall, width), f32),
            pltpu.VMEM((3, rows, width), f32),
            pltpu.VMEM((slabs, EDGE, width), f32),
            pltpu.VMEM((slabs, EDGE, width), f32),
            pltpu.VMEM(((slabs + 3) // 4, EDGE, width), f32),
            pltpu.VMEM(((slabs + 3) // 4, EDGE, width), f32),
            pltpu.VMEM((slabs, rows, width), f32),
            pltpu.VMEM((slabs, rows // 4, width), f32),
            pltpu.VMEM((slabs, rows, width), f32),
            pltpu.VMEM((slabs, rows // 4, width), f32),
            dma((4,)), dma((16,)), dma((16,)),
            dma((slabs,)), dma((slabs,)), dma((slabs,)), dma((slabs,)),
        ],
        compiler_params=pltpu.CompilerParams(
            collective_id=0, has_side_effects=True, vmem_limit_bytes=60 * 1024 * 1024
        ),
        cost_estimate=pl.CostEstimate(
            flops=50_000_000, bytes_accessed=800_000, transcendentals=0
        ),
    )(
        fluid_state.reshape(slabs, rows, width),
        velocity.reshape(vels, rows, width),
        shifts.reshape(1, rows),
        fraction.reshape(1, rows),
    )
    return result.reshape(fields, layers, rows, width)


def solution(mesh):
    return jax.shard_map(
        on_device,
        mesh=mesh,
        in_specs=(P(None, None, "rad", "az"), P(None, None, "rad", "az"), P("rad"), P("rad")),
        out_specs=P(None, None, "rad", "az"),
        check_vma=False,
    )
```

```python
import functools

import jax
import jax.numpy as jnp
from jax import lax
from jax.experimental import pallas as pl
from jax.experimental.pallas import tpu as pltpu
from jax.sharding import PartitionSpec as P

STEPS = 2
EDGE = 8
NINE = 9


def kernel(
    n_az, n_rad, fields, layers,
    fluid, vel, shift_hbm, frac_hbm, out,
    shift_ref, frac_ref, shift_b, weight_b, xin, own_lo, own_hi, row_lo, row_hi, halo_l, halo_r, halo_d, halo_u,
    coef, coef_s, coef_t, seam, brim, got_brim, brim_tail, got_brim_tail, rot, tail, got, got_tail, relayed,
    in_sem, send_h, recv_h, send_a, recv_a, send_b, recv_b, send_f, recv_f,
):
    slabs = fields * layers
    vels = 2 * layers
    total = slabs + vels
    rows, width = xin.shape[1], xin.shape[2]
    tall = rows + 2 * EDGE
    az = lax.axis_index("az")
    rad = lax.axis_index("rad")
    right = lax.rem(az + 1, n_az)
    right2 = lax.rem(az + 2, n_az)
    left = lax.rem(az + n_az - 1, n_az)
    left2 = lax.rem(az + n_az - 2, n_az)
    has_dn = rad > 0
    has_up = rad < n_rad - 1

    def dev(a, r):
        return {"az": a, "rad": r}

    load_f = pltpu.make_async_copy(fluid, xin.at[pl.ds(0, slabs)], in_sem.at[0])
    load_v = pltpu.make_async_copy(vel, xin.at[pl.ds(slabs, vels)], in_sem.at[1])
    load_s = pltpu.make_async_copy(shift_hbm, shift_ref, in_sem.at[2])
    load_w = pltpu.make_async_copy(frac_hbm, frac_ref, in_sem.at[3])
    loads = (load_s, load_w, load_f, load_v)
    for c in loads:
        c.start()

    barrier = pltpu.get_barrier_semaphore()
    for a in (left, right, left2):
        pl.semaphore_signal(barrier, inc=1, device_id=dev(a, rad))

    @pl.when(has_dn)
    def _():
        for a in (left, az, right):
            pl.semaphore_signal(barrier, inc=1, device_id=dev(a, rad - 1))

    @pl.when(has_up)
    def _():
        for a in (left, az, right):
            pl.semaphore_signal(barrier, inc=1, device_id=dev(a, rad + 1))

    quarter = width // 4
    rows4 = rows // 4

    def iota(shape, axis):
        return lax.broadcasted_iota(jnp.int32, shape, axis)

    sub8 = iota((EDGE, width), 0)
    lane_r = iota((rows, width), 1)
    half = EDGE // 2
    own = pl.ds(EDGE, rows)

    for c in loads:
        c.wait()

    for i in range(total // 2):
        a, b = xin[2 * i, rows - EDGE :, :], xin[2 * i + 1, rows - EDGE :, :]
        row_hi[i] = jnp.where(sub8 >= half, a, pltpu.roll(b, half, 0))
        a, b = xin[2 * i, :EDGE, :], xin[2 * i + 1, :EDGE, :]
        row_lo[i] = jnp.where(sub8 < half, a, pltpu.roll(b, half, 0))
    lo = xin[0]
    hi = pltpu.roll(xin[0], NINE, 1)
    for j in range(1, total):
        x = xin[j]
        mine = lane_r >= NINE * j
        hi = jnp.where(mine, pltpu.roll(x, (NINE * (j + 1)) % width, 1), hi)
        lo = jnp.where(mine, pltpu.roll(x, NINE * j, 1), lo)
    own_hi[own, :] = hi
    own_lo[own, :] = lo

    def prev(x, axis):
        return pltpu.roll(x, 1, axis)

    def nxt(x, axis):
        return pltpu.roll(x, x.shape[axis] - 1, axis)

    def coefficients(vr, va, keep):
        face_r = 0.5 * (prev(vr, 0) + vr)
        face_a = 0.5 * (prev(va, 1) + va)
        rp, rm = jnp.maximum(face_r, 0.0), jnp.minimum(face_r, 0.0)
        ap, am = jnp.maximum(face_a, 0.0), jnp.minimum(face_a, 0.0)
        mid_c = 1.0 + ((rm - nxt(rp, 0)) + (am - nxt(ap, 1)))
        all5 = [mid_c, rp, -nxt(rm, 0), ap, -nxt(am, 1)]
        if keep is not None:
            all5 = [jnp.where(keep, c, 0.0) for c in all5]
        return all5

    def transport(values, pick):
        def stencil(n, x):
            return (
                (pick(n, 0) * x + pick(n, 1) * prev(x, 0))
                + (pick(n, 2) * nxt(x, 0) + pick(n, 3) * prev(x, 1))
                + pick(n, 4) * nxt(x, 1)
            )

        for _ in range(STEPS):
            once = [stencil(n, x) for n, x in enumerate(values)]
            twice = [stencil(n, x) for n, x in enumerate(once)]
            values = [0.5 * (x + t) for x, t in zip(values, twice)]
        return values

    for layer in range(layers):
        cs = coefficients(xin[slabs + layer], xin[slabs + layers + layer], None)
        for k in range(5):
            coef[layer, k] = cs[k]

    pick_row = iota((rows, rows), 0) == iota((rows, rows), 1)

    def to_rows(ref):
        spread = jnp.broadcast_to(ref[...].astype(jnp.float32), (rows, rows))
        return jnp.sum(jnp.where(pick_row, spread, 0.0), axis=1, keepdims=True)

    shift_b[...] = jnp.broadcast_to(to_rows(shift_ref).astype(jnp.int32), (rows, width))
    weight_b[...] = jnp.broadcast_to(to_rows(frac_ref), (rows, width))

    pl.semaphore_wait(
        barrier, 3 + 3 * has_dn.astype(jnp.int32) + 3 * has_up.astype(jnp.int32)
    )

    def remote(src, dst, k, a, r):
        return pltpu.make_async_remote_copy(
            src_ref=src, dst_ref=dst, send_sem=send_h.at[k], recv_sem=recv_h.at[k],
            device_id=dev(a, r), device_id_type=pl.DeviceIdType.MESH,
        )

    top = pl.ds(rows, EDGE)
    bottom = pl.ds(EDGE, EDGE)
    after = pl.ds(EDGE + rows, EDGE)
    before = pl.ds(0, EDGE)
    to_up = [
        remote(own_hi.at[top], halo_l.at[before], 3, right, rad + 1),
        remote(own_lo.at[top], halo_r.at[before], 4, left, rad + 1),
        remote(own_hi.at[top], own_hi.at[before], 8, az, rad + 1),
        remote(own_lo.at[top], own_lo.at[before], 9, az, rad + 1),
        remote(row_hi, halo_d, 2, az, rad + 1),
    ]
    to_dn = [
        remote(own_hi.at[bottom], halo_l.at[after], 6, right, rad - 1),
        remote(own_lo.at[bottom], halo_r.at[after], 7, left, rad - 1),
        remote(own_hi.at[bottom], own_hi.at[after], 10, az, rad - 1),
        remote(own_lo.at[bottom], own_lo.at[after], 11, az, rad - 1),
        remote(row_lo, halo_u, 5, az, rad - 1),
    ]
    sides = [
        remote(own_hi.at[own], halo_l.at[own], 0, right, rad),
        remote(own_lo.at[own], halo_r.at[own], 1, left, rad),
    ]
    for c in sides:
        c.start()

    @pl.when(has_up)
    def _():
        for c in to_up:
            c.start()

    @pl.when(has_dn)
    def _():
        for c in to_dn:
            c.start()

    def send_a_of(j):
        return pltpu.make_async_remote_copy(
            src_ref=rot.at[j], dst_ref=got.at[j], send_sem=send_a.at[j], recv_sem=recv_a.at[j],
            device_id=dev(right, rad), device_id_type=pl.DeviceIdType.MESH,
        )

    def send_b_of(j):
        return pltpu.make_async_remote_copy(
            src_ref=tail.at[j], dst_ref=got_tail.at[j], send_sem=send_b.at[j], recv_sem=recv_b.at[j],
            device_id=dev(right2, rad), device_id_type=pl.DeviceIdType.MESH,
        )


    even = lax.rem(az, 2) == 0
    is_even = jnp.full((rows, width), lax.rem(az, 2), jnp.int32) == 0

    def relay_of(j):
        return pltpu.make_async_remote_copy(
            src_ref=got.at[j], dst_ref=relayed.at[j], send_sem=send_f.at[j], recv_sem=recv_f.at[j],
            device_id=dev(right, rad), device_id_type=pl.DeviceIdType.MESH,
        )

    def take(x, index):
        return jnp.take_along_axis(x, index, axis=1, mode="promise_in_bounds")

    weight, shift = weight_b[...], shift_b[...]
    source = (lane_r - shift) & (width - 1)
    lane_q = lane_r[:rows4]

    def interior(layer, carry):
        values = [xin[f * layers + layer] for f in range(fields)]
        values = transport(values, lambda n, k: coef[layer, k])
        for f, v in enumerate(values):
            j = f * layers + layer
            y = (1.0 - weight) * v + weight * prev(v, 1)
            turned = take(y, source)
            rot[j] = turned
            send_a_of(j).start()
            packed = turned[:rows4]
            for q in range(1, 4):
                part = pltpu.roll(turned[q * rows4 : (q + 1) * rows4], q * quarter, 1)
                packed = jnp.where(lane_q >= q * quarter, part, packed)
            tail[j] = packed
        return carry

    lax.fori_loop(0, layers, interior, 0)

    for c in sides:
        c.wait()

    @pl.when(has_dn)
    def _():
        for c in to_up:
            c.wait_recv()
        for c in to_dn:
            c.wait_send()

    @pl.when(has_up)
    def _():
        for c in to_dn:
            c.wait_recv()
        for c in to_up:
            c.wait_send()

    row_s = iota((4 * EDGE, width), 0)
    keep_s = jnp.logical_and(
        jnp.logical_or(row_s >= EDGE, has_dn), jnp.logical_or(row_s < 3 * EDGE, has_up)
    )

    def strip(j):
        below, above = halo_d[j // 2], halo_u[j // 2]
        if j % 2:
            below, above = pltpu.roll(below, half, 0), pltpu.roll(above, half, 0)
        both = jnp.concatenate([below, xin[j, :EDGE], xin[j, rows - EDGE :], above], axis=0)
        return jnp.where(keep_s, both, 0.0)

    for layer in range(layers):
        cs = coefficients(strip(slabs + layer), strip(slabs + layers + layer), keep_s)
        for k in range(5):
            coef_s[layer, k] = cs[k]

    lane_t = iota((tall, width), 1)
    row_t = iota((tall, width), 0)
    keep_t = jnp.logical_and(
        jnp.logical_or(row_t >= EDGE, has_dn), jnp.logical_or(row_t < EDGE + rows, has_up)
    )
    k16 = lane_t & 15
    group = lane_t >> 4
    on_right = (group & 1) == 1
    layer_of = (group >> 1) & 1
    part_of = group >> 2
    lag = NINE - 7
    offset = jnp.where(
        on_right,
        jnp.where(k16 < NINE, k16, k16 - NINE),
        jnp.where(k16 < 7, k16 + lag, k16 - 7),
    )
    use_l = jnp.logical_and(jnp.logical_not(on_right), k16 < 7)
    use_r = jnp.logical_and(on_right, k16 >= NINE)

    def columns(slab):
        index = NINE * slab + offset
        mine = jnp.where(on_right, take(own_hi[...], index), take(own_lo[...], index))
        x = jnp.where(use_l, take(halo_l[...], index), mine)
        x = jnp.where(use_r, take(halo_r[...], index), x)
        return jnp.where(keep_t, x, 0.0)

    cs = coefficients(
        columns(slabs + layer_of), columns(slabs + layers + layer_of), keep_t
    )
    for k in range(5):
        coef_t[k] = cs[k]

    tiles = (fields + 1) // 2
    cols = [
        columns(jnp.minimum(2 * t + part_of, fields - 1) * layers + layer_of)
        for t in range(tiles)
    ]
    cols = transport(cols, lambda n, k: coef_t[k])
    cols_y = []
    for v in cols:
        v, p = v[EDGE : EDGE + rows], prev(v, 1)[EDGE : EDGE + rows]
        cols_y.append((1.0 - weight) * v + weight * p)

    slab_l = (lane_r * 57) >> 9
    m9 = lane_r - NINE * slab_l
    field_l, layer_l = slab_l // layers, slab_l % layers
    at = 64 * (field_l & 1) + 32 * layer_l + jnp.where(m9 < 5, m9 + 7, m9 + 16)
    at = at & (width - 1)
    s_tile = take(cols_y[tiles - 1], at)
    for t in range(tiles - 2, -1, -1):
        s_tile = jnp.where(field_l < 2 * (t + 1), take(cols_y[t], at), s_tile)
    seam[0] = s_tile

    first = sub8 < half

    def outer(x):
        return jnp.where(first, x[:EDGE], x[rows - EDGE :])

    w8, source8, lane8 = outer(weight), outer(source), iota((EDGE, width), 1)
    shift8 = outer(shift)
    spare = [None] * slabs
    for layer in range(layers):
        js = [f * layers + layer for f in range(fields)]
        values = transport([strip(j) for j in js], lambda n, k: coef_s[layer, k])
        for j, v in zip(js, values):
            p = prev(v, 1)
            v8 = jnp.where(first, v[EDGE : 2 * EDGE], v[2 * EDGE : 3 * EDGE])
            p8 = jnp.where(first, p[EDGE : 2 * EDGE], p[2 * EDGE : 3 * EDGE])
            spare[j] = take((1.0 - w8) * v8 + w8 * p8, source8)
            brim[j] = spare[j]
    groups = (slabs + 3) // 4
    for u in range(groups):
        packed = spare[4 * u]
        for q in range(1, min(4, slabs - 4 * u)):
            packed = jnp.where(
                lane8 >= q * quarter, pltpu.roll(spare[4 * u + q], q * quarter, 1), packed
            )
        brim_tail[u] = packed

    late = [
        remote(seam.at[0], seam.at[1], 12, right, rad),
        remote(brim, got_brim, 13, right, rad),
        remote(seam.at[0], seam.at[2], 14, right2, rad),
        remote(brim_tail, got_brim_tail, 15, right2, rad),
    ]
    for c in late:
        c.start()

    @pl.when(even)
    def _():
        for j in range(slabs):
            send_b_of(j).start()

    in_strip = jnp.logical_or(source <= 4, source >= width - 4)
    seam_lane = jnp.where(source <= 4, source, source - (width - NINE))
    here, next_ = lane_r >= shift, lane_r >= shift - width
    here8, next8 = lane8 >= shift8, lane8 >= shift8 - width

    def relay(j, carry):
        send_a_of(j).wait_recv()

        @pl.when(even)
        def _():
            relay_of(j).start()

        return carry

    lax.fori_loop(0, slabs, relay, 0)

    def gather(j, carry):
        @pl.when(even)
        def _():
            send_b_of(j).wait_recv()

        @pl.when(jnp.logical_not(even))
        def _():
            relay_of(j).wait_recv()

        b = got_tail[j]
        parts = [b] + [pltpu.roll(b, width - q * quarter, 1) for q in range(1, 4)]
        far = jnp.where(is_even, jnp.concatenate(parts, axis=0), relayed[j])
        out[j] = jnp.where(here, rot[j], jnp.where(next_, got[j], far))
        return carry

    lax.fori_loop(0, slabs, gather, 0)
    for c in late:
        c.wait_recv()

    for j in range(slabs):
        at = (NINE * j + seam_lane) & (width - 1)
        patch = jnp.where(
            here, take(seam[0], at), jnp.where(next_, take(seam[1], at), take(seam[2], at))
        )
        q = j % 4
        far8 = got_brim_tail[j // 4]
        if q:
            far8 = pltpu.roll(far8, width - q * quarter, 1)
        rim = jnp.where(here8, brim[j], jnp.where(next8, got_brim[j], far8))
        base = jnp.concatenate(
            [
                jnp.where(first, rim, out[j, :EDGE]),
                out[j, EDGE : rows - EDGE],
                jnp.where(first, out[j, rows - EDGE :], rim),
            ],
            axis=0,
        )
        out[j] = jnp.where(in_strip, patch, base)

    for c in late:
        c.wait_send()

    def drain(j, carry):
        send_a_of(j).wait_send()

        @pl.when(even)
        def _():
            send_b_of(j).wait_send()
            relay_of(j).wait_send()

        return carry

    lax.fori_loop(0, slabs, drain, 0)


def on_device(fluid_state, velocity, shifts, fraction):
    fields, layers, rows, width = fluid_state.shape
    n_az, n_rad = lax.axis_size("az"), lax.axis_size("rad")
    slabs, vels = fields * layers, 2 * layers
    total = slabs + vels
    tall = rows + 2 * EDGE
    f32 = jnp.float32
    dma = pltpu.SemaphoreType.DMA
    hbm = pl.BlockSpec(memory_space=pltpu.HBM)
    vmem = pl.BlockSpec(memory_space=pltpu.VMEM)
    result = pl.pallas_call(
        functools.partial(kernel, n_az, n_rad, fields, layers),
        out_shape=pltpu.VMEM((slabs, rows, width), f32),
        in_specs=[hbm, hbm, hbm, hbm],
        out_specs=vmem,
        scratch_shapes=[
            pltpu.VMEM((1, rows), jnp.int32),
            pltpu.VMEM((1, rows), f32),
            pltpu.VMEM((rows, width), jnp.int32),
            pltpu.VMEM((rows, width), f32),
            pltpu.VMEM((total, rows, width), f32),
            pltpu.VMEM((tall, width), f32),
            pltpu.VMEM((tall, width), f32),
            pltpu.VMEM((total // 2, EDGE, width), f32),
            pltpu.VMEM((total // 2, EDGE, width), f32),
            pltpu.VMEM((tall, width), f32),
            pltpu.VMEM((tall, width), f32),
            pltpu.VMEM((total // 2, EDGE, width), f32),
            pltpu.VMEM((total // 2, EDGE, width), f32),
            pltpu.VMEM((layers, 5, rows, width), f32),
            pltpu.VMEM((layers, 5, 4 * EDGE, width), f32),
            pltpu.VMEM((5, tall, width), f32),
            pltpu.VMEM((3, rows, width), f32),
            pltpu.VMEM((slabs, EDGE, width), f32),
            pltpu.VMEM((slabs, EDGE, width), f32),
            pltpu.VMEM(((slabs + 3) // 4, EDGE, width), f32),
            pltpu.VMEM(((slabs + 3) // 4, EDGE, width), f32),
            pltpu.VMEM((slabs, rows, width), f32),
            pltpu.VMEM((slabs, rows // 4, width), f32),
            pltpu.VMEM((slabs, rows, width), f32),
            pltpu.VMEM((slabs, rows // 4, width), f32),
            pltpu.VMEM((slabs, rows, width), f32),
            dma((4,)), dma((16,)), dma((16,)),
            dma((slabs,)), dma((slabs,)), dma((slabs,)), dma((slabs,)), dma((slabs,)), dma((slabs,)),
        ],
        compiler_params=pltpu.CompilerParams(
            collective_id=0, has_side_effects=True, vmem_limit_bytes=60 * 1024 * 1024
        ),
        cost_estimate=pl.CostEstimate(
            flops=50_000_000, bytes_accessed=800_000, transcendentals=0
        ),
    )(
        fluid_state.reshape(slabs, rows, width),
        velocity.reshape(vels, rows, width),
        shifts.reshape(1, rows),
        fraction.reshape(1, rows),
    )
    return result.reshape(fields, layers, rows, width)


def solution(mesh):
    return jax.shard_map(
        on_device,
        mesh=mesh,
        in_specs=(P(None, None, "rad", "az"), P(None, None, "rad", "az"), P("rad"), P("rad")),
        out_specs=P(None, None, "rad", "az"),
        check_vma=False,
    )
```

```python
import functools

import jax
import jax.numpy as jnp
from jax import lax
from jax.experimental import pallas as pl
from jax.experimental.pallas import tpu as pltpu
from jax.sharding import PartitionSpec as P

STEPS = 2
EDGE = 8
NINE = 9


def kernel(
    n_az, n_rad, fields, layers,
    fluid, vel, shift_hbm, frac_hbm, out,
    shift_ref, frac_ref, shift_b, weight_b, xin, own_lo, own_hi, row_lo, row_hi, halo_l, halo_r, halo_d, halo_u,
    coef, coef_s, coef_t, seam, brim, got_brim, brim_tail, got_brim_tail, rot, tail, got, got_tail, relayed,
    in_sem, send_h, recv_h, send_a, recv_a, send_b, recv_b, send_f, recv_f,
):
    slabs = fields * layers
    vels = 2 * layers
    total = slabs + vels
    rows, width = xin.shape[1], xin.shape[2]
    tall = rows + 2 * EDGE
    az = lax.axis_index("az")
    rad = lax.axis_index("rad")
    right = lax.rem(az + 1, n_az)
    right2 = lax.rem(az + 2, n_az)
    left = lax.rem(az + n_az - 1, n_az)
    left2 = lax.rem(az + n_az - 2, n_az)
    has_dn = rad > 0
    has_up = rad < n_rad - 1

    def dev(a, r):
        return {"az": a, "rad": r}

    load_f = pltpu.make_async_copy(fluid, xin.at[pl.ds(0, slabs)], in_sem.at[0])
    load_v = pltpu.make_async_copy(vel, xin.at[pl.ds(slabs, vels)], in_sem.at[1])
    load_s = pltpu.make_async_copy(shift_hbm, shift_ref, in_sem.at[2])
    load_w = pltpu.make_async_copy(frac_hbm, frac_ref, in_sem.at[3])
    loads = (load_s, load_w, load_f, load_v)
    for c in loads:
        c.start()

    barrier = pltpu.get_barrier_semaphore()
    for a in (left, right, left2):
        pl.semaphore_signal(barrier, inc=1, device_id=dev(a, rad))

    @pl.when(has_dn)
    def _():
        for a in (left, az, right):
            pl.semaphore_signal(barrier, inc=1, device_id=dev(a, rad - 1))

    @pl.when(has_up)
    def _():
        for a in (left, az, right):
            pl.semaphore_signal(barrier, inc=1, device_id=dev(a, rad + 1))

    quarter = width // 4
    rows4 = rows // 4

    def iota(shape, axis):
        return lax.broadcasted_iota(jnp.int32, shape, axis)

    sub8 = iota((EDGE, width), 0)
    lane_r = iota((rows, width), 1)
    half = EDGE // 2
    own = pl.ds(EDGE, rows)

    for c in loads:
        c.wait()

    for i in range(total // 2):
        a, b = xin[2 * i, rows - EDGE :, :], xin[2 * i + 1, rows - EDGE :, :]
        row_hi[i] = jnp.where(sub8 >= half, a, pltpu.roll(b, half, 0))
        a, b = xin[2 * i, :EDGE, :], xin[2 * i + 1, :EDGE, :]
        row_lo[i] = jnp.where(sub8 < half, a, pltpu.roll(b, half, 0))
    lo = xin[0]
    hi = pltpu.roll(xin[0], NINE, 1)
    for j in range(1, total):
        x = xin[j]
        mine = lane_r >= NINE * j
        hi = jnp.where(mine, pltpu.roll(x, (NINE * (j + 1)) % width, 1), hi)
        lo = jnp.where(mine, pltpu.roll(x, NINE * j, 1), lo)
    own_hi[own, :] = hi
    own_lo[own, :] = lo

    def prev(x, axis):
        return pltpu.roll(x, 1, axis)

    def nxt(x, axis):
        return pltpu.roll(x, x.shape[axis] - 1, axis)

    def coefficients(vr, va, keep):
        face_r = 0.5 * (prev(vr, 0) + vr)
        face_a = 0.5 * (prev(va, 1) + va)
        rp, rm = jnp.maximum(face_r, 0.0), jnp.minimum(face_r, 0.0)
        ap, am = jnp.maximum(face_a, 0.0), jnp.minimum(face_a, 0.0)
        mid_c = 1.0 + ((rm - nxt(rp, 0)) + (am - nxt(ap, 1)))
        all5 = [mid_c, rp, -nxt(rm, 0), ap, -nxt(am, 1)]
        if keep is not None:
            all5 = [jnp.where(keep, c, 0.0) for c in all5]
        return all5

    def transport(values, pick):
        def stencil(n, x):
            return (
                (pick(n, 0) * x + pick(n, 1) * prev(x, 0))
                + (pick(n, 2) * nxt(x, 0) + pick(n, 3) * prev(x, 1))
                + pick(n, 4) * nxt(x, 1)
            )

        for _ in range(STEPS):
            once = [stencil(n, x) for n, x in enumerate(values)]
            twice = [stencil(n, x) for n, x in enumerate(once)]
            values = [0.5 * (x + t) for x, t in zip(values, twice)]
        return values

    for layer in range(layers):
        cs = coefficients(xin[slabs + layer], xin[slabs + layers + layer], None)
        for k in range(5):
            coef[layer, k] = cs[k]

    pick_row = iota((rows, rows), 0) == iota((rows, rows), 1)

    def to_rows(ref):
        spread = jnp.broadcast_to(ref[...].astype(jnp.float32), (rows, rows))
        return jnp.sum(jnp.where(pick_row, spread, 0.0), axis=1, keepdims=True)

    shift_b[...] = jnp.broadcast_to(to_rows(shift_ref).astype(jnp.int32), (rows, width))
    weight_b[...] = jnp.broadcast_to(to_rows(frac_ref), (rows, width))

    pl.semaphore_wait(
        barrier, 3 + 3 * has_dn.astype(jnp.int32) + 3 * has_up.astype(jnp.int32)
    )

    def remote(src, dst, k, a, r):
        return pltpu.make_async_remote_copy(
            src_ref=src, dst_ref=dst, send_sem=send_h.at[k], recv_sem=recv_h.at[k],
            device_id=dev(a, r), device_id_type=pl.DeviceIdType.MESH,
        )

    top = pl.ds(rows, EDGE)
    bottom = pl.ds(EDGE, EDGE)
    after = pl.ds(EDGE + rows, EDGE)
    before = pl.ds(0, EDGE)
    to_up = [
        remote(own_hi.at[top], halo_l.at[before], 3, right, rad + 1),
        remote(own_lo.at[top], halo_r.at[before], 4, left, rad + 1),
        remote(own_hi.at[top], own_hi.at[before], 8, az, rad + 1),
        remote(own_lo.at[top], own_lo.at[before], 9, az, rad + 1),
        remote(row_hi, halo_d, 2, az, rad + 1),
    ]
    to_dn = [
        remote(own_hi.at[bottom], halo_l.at[after], 6, right, rad - 1),
        remote(own_lo.at[bottom], halo_r.at[after], 7, left, rad - 1),
        remote(own_hi.at[bottom], own_hi.at[after], 10, az, rad - 1),
        remote(own_lo.at[bottom], own_lo.at[after], 11, az, rad - 1),
        remote(row_lo, halo_u, 5, az, rad - 1),
    ]
    sides = [
        remote(own_hi.at[own], halo_l.at[own], 0, right, rad),
        remote(own_lo.at[own], halo_r.at[own], 1, left, rad),
    ]
    for c in sides:
        c.start()

    @pl.when(has_up)
    def _():
        for c in to_up:
            c.start()

    @pl.when(has_dn)
    def _():
        for c in to_dn:
            c.start()

    def send_a_of(j):
        return pltpu.make_async_remote_copy(
            src_ref=rot.at[j], dst_ref=got.at[j], send_sem=send_a.at[j], recv_sem=recv_a.at[j],
            device_id=dev(right, rad), device_id_type=pl.DeviceIdType.MESH,
        )

    def send_b_of(j):
        return pltpu.make_async_remote_copy(
            src_ref=tail.at[j], dst_ref=got_tail.at[j], send_sem=send_b.at[j], recv_sem=recv_b.at[j],
            device_id=dev(right2, rad), device_id_type=pl.DeviceIdType.MESH,
        )


    even = lax.rem(az, 2) == 0
    is_even = jnp.full((rows, width), lax.rem(az, 2), jnp.int32) == 0

    def relay_of(j):
        return pltpu.make_async_remote_copy(
            src_ref=got.at[j], dst_ref=relayed.at[j], send_sem=send_f.at[j], recv_sem=recv_f.at[j],
            device_id=dev(right, rad), device_id_type=pl.DeviceIdType.MESH,
        )

    def take(x, index):
        return jnp.take_along_axis(x, index, axis=1, mode="promise_in_bounds")

    weight, shift = weight_b[...], shift_b[...]
    source = (lane_r - shift) & (width - 1)
    lane_q = lane_r[:rows4]

    def interior(layer, carry):
        values = [xin[f * layers + layer] for f in range(fields)]
        values = transport(values, lambda n, k: coef[layer, k])
        for f, v in enumerate(values):
            j = f * layers + layer
            y = (1.0 - weight) * v + weight * prev(v, 1)
            turned = take(y, source)
            rot[j] = turned
            send_a_of(j).start()
            packed = turned[:rows4]
            for q in range(1, 4):
                part = pltpu.roll(turned[q * rows4 : (q + 1) * rows4], q * quarter, 1)
                packed = jnp.where(lane_q >= q * quarter, part, packed)
            tail[j] = packed
        return carry

    lax.fori_loop(0, layers, interior, 0)

    corner_up, corner_dn = to_up.pop(1), to_dn.pop(1)
    sides[0].wait_recv()

    @pl.when(has_dn)
    def _():
        for c in to_up:
            c.wait_recv()

    @pl.when(has_up)
    def _():
        for c in to_dn:
            c.wait_recv()

    row_s = iota((4 * EDGE, width), 0)
    keep_s = jnp.logical_and(
        jnp.logical_or(row_s >= EDGE, has_dn), jnp.logical_or(row_s < 3 * EDGE, has_up)
    )

    def strip(j):
        below, above = halo_d[j // 2], halo_u[j // 2]
        if j % 2:
            below, above = pltpu.roll(below, half, 0), pltpu.roll(above, half, 0)
        both = jnp.concatenate([below, xin[j, :EDGE], xin[j, rows - EDGE :], above], axis=0)
        return jnp.where(keep_s, both, 0.0)

    for layer in range(layers):
        cs = coefficients(strip(slabs + layer), strip(slabs + layers + layer), keep_s)
        for k in range(5):
            coef_s[layer, k] = cs[k]

    lane_t = iota((tall, width), 1)
    row_t = iota((tall, width), 0)
    keep_t = jnp.logical_and(
        jnp.logical_or(row_t >= EDGE, has_dn), jnp.logical_or(row_t < EDGE + rows, has_up)
    )
    k32 = lane_t & 31
    group = lane_t >> 5
    layer_of = group & 1
    part_of = group >> 1
    lower = k32 < NINE
    offset = jnp.where(lower, k32, k32 - NINE)
    tiles = (fields + 1) // 2

    def seam_columns(before_ref, after_ref, side):
        def columns(slab):
            index = (NINE * slab + offset) & (width - 1)
            x = jnp.where(lower, take(before_ref[...], index), take(after_ref[...], index))
            return jnp.where(keep_t, x, 0.0)

        cs = coefficients(
            columns(slabs + layer_of), columns(slabs + layers + layer_of), keep_t
        )
        for k in range(5):
            coef_t[side, k] = cs[k]
        cols = [
            columns(jnp.minimum(2 * t + part_of, fields - 1) * layers + layer_of)
            for t in range(tiles)
        ]
        cols = transport(cols, lambda n, k: coef_t[side, k])
        cols_y = []
        for v in cols:
            v, p = v[EDGE : EDGE + rows], prev(v, 1)[EDGE : EDGE + rows]
            cols_y.append((1.0 - weight) * v + weight * p)
        return cols_y

    slab_l = (lane_r * 57) >> 9
    m9 = lane_r - NINE * slab_l
    field_l, layer_l = slab_l // layers, slab_l % layers

    def seam_tile(cols_y, first_k):
        at = (64 * (field_l & 1) + 32 * layer_l + m9 + first_k) & (width - 1)
        x = take(cols_y[tiles - 1], at)
        for t in range(tiles - 2, -1, -1):
            x = jnp.where(field_l < 2 * (t + 1), take(cols_y[t], at), x)
        return x

    seam[0] = seam_tile(seam_columns(halo_l, own_lo, 0), 5)

    first = sub8 < half

    def outer(x):
        return jnp.where(first, x[:EDGE], x[rows - EDGE :])

    w8, source8, lane8 = outer(weight), outer(source), iota((EDGE, width), 1)
    shift8 = outer(shift)
    spare = [None] * slabs
    for layer in range(layers):
        js = [f * layers + layer for f in range(fields)]
        values = transport([strip(j) for j in js], lambda n, k: coef_s[layer, k])
        for j, v in zip(js, values):
            p = prev(v, 1)
            v8 = jnp.where(first, v[EDGE : 2 * EDGE], v[2 * EDGE : 3 * EDGE])
            p8 = jnp.where(first, p[EDGE : 2 * EDGE], p[2 * EDGE : 3 * EDGE])
            spare[j] = take((1.0 - w8) * v8 + w8 * p8, source8)
            brim[j] = spare[j]
    groups = (slabs + 3) // 4
    for u in range(groups):
        packed = spare[4 * u]
        for q in range(1, min(4, slabs - 4 * u)):
            packed = jnp.where(
                lane8 >= q * quarter, pltpu.roll(spare[4 * u + q], q * quarter, 1), packed
            )
        brim_tail[u] = packed

    late = [
        remote(seam.at[0], seam.at[1], 12, right, rad),
        remote(brim, got_brim, 13, right, rad),
        remote(brim_tail, got_brim_tail, 15, right2, rad),
    ]
    for c in late:
        c.start()

    @pl.when(even)
    def _():
        for j in range(slabs):
            send_b_of(j).start()

    sides[1].wait_recv()

    @pl.when(has_dn)
    def _():
        corner_up.wait_recv()
        for c in to_dn + [corner_dn]:
            c.wait_send()

    @pl.when(has_up)
    def _():
        corner_dn.wait_recv()
        for c in to_up + [corner_up]:
            c.wait_send()

    for c in sides:
        c.wait_send()
    seam[2] = seam_tile(seam_columns(own_hi, halo_r, 1), 0)

    in_strip = jnp.logical_or(source <= 4, source >= width - 4)
    here, next_ = lane_r >= shift, lane_r >= shift - width
    low = source <= 4
    seam_lane = jnp.where(
        low, source + 4, jnp.where(here, source - (width - NINE), source - (width - 4))
    )
    at_end = jnp.logical_and(here, jnp.logical_not(low))
    mine = jnp.logical_or(
        jnp.logical_and(here, low),
        jnp.logical_and(jnp.logical_not(jnp.logical_or(here, low)), next_),
    )
    here8, next8 = lane8 >= shift8, lane8 >= shift8 - width

    def relay(j, carry):
        send_a_of(j).wait_recv()

        @pl.when(even)
        def _():
            relay_of(j).start()

        return carry

    lax.fori_loop(0, slabs, relay, 0)

    def gather(j, carry):
        @pl.when(even)
        def _():
            send_b_of(j).wait_recv()

        @pl.when(jnp.logical_not(even))
        def _():
            relay_of(j).wait_recv()

        b = got_tail[j]
        parts = [b] + [pltpu.roll(b, width - q * quarter, 1) for q in range(1, 4)]
        far = jnp.where(is_even, jnp.concatenate(parts, axis=0), relayed[j])
        out[j] = jnp.where(here, rot[j], jnp.where(next_, got[j], far))
        return carry

    lax.fori_loop(0, slabs, gather, 0)
    for c in late:
        c.wait_recv()

    for j in range(slabs):
        at = (NINE * j + seam_lane) & (width - 1)
        patch = jnp.where(
            mine, take(seam[0], at), jnp.where(at_end, take(seam[2], at), take(seam[1], at))
        )
        q = j % 4
        far8 = got_brim_tail[j // 4]
        if q:
            far8 = pltpu.roll(far8, width - q * quarter, 1)
        rim = jnp.where(here8, brim[j], jnp.where(next8, got_brim[j], far8))
        base = jnp.concatenate(
            [
                jnp.where(first, rim, out[j, :EDGE]),
                out[j, EDGE : rows - EDGE],
                jnp.where(first, out[j, rows - EDGE :], rim),
            ],
            axis=0,
        )
        out[j] = jnp.where(in_strip, patch, base)

    for c in late:
        c.wait_send()

    def drain(j, carry):
        send_a_of(j).wait_send()

        @pl.when(even)
        def _():
            send_b_of(j).wait_send()
            relay_of(j).wait_send()

        return carry

    lax.fori_loop(0, slabs, drain, 0)


def on_device(fluid_state, velocity, shifts, fraction):
    fields, layers, rows, width = fluid_state.shape
    n_az, n_rad = lax.axis_size("az"), lax.axis_size("rad")
    slabs, vels = fields * layers, 2 * layers
    total = slabs + vels
    tall = rows + 2 * EDGE
    f32 = jnp.float32
    dma = pltpu.SemaphoreType.DMA
    hbm = pl.BlockSpec(memory_space=pltpu.HBM)
    vmem = pl.BlockSpec(memory_space=pltpu.VMEM)
    result = pl.pallas_call(
        functools.partial(kernel, n_az, n_rad, fields, layers),
        out_shape=pltpu.VMEM((slabs, rows, width), f32),
        in_specs=[hbm, hbm, hbm, hbm],
        out_specs=vmem,
        scratch_shapes=[
            pltpu.VMEM((1, rows), jnp.int32),
            pltpu.VMEM((1, rows), f32),
            pltpu.VMEM((rows, width), jnp.int32),
            pltpu.VMEM((rows, width), f32),
            pltpu.VMEM((total, rows, width), f32),
            pltpu.VMEM((tall, width), f32),
            pltpu.VMEM((tall, width), f32),
            pltpu.VMEM((total // 2, EDGE, width), f32),
            pltpu.VMEM((total // 2, EDGE, width), f32),
            pltpu.VMEM((tall, width), f32),
            pltpu.VMEM((tall, width), f32),
            pltpu.VMEM((total // 2, EDGE, width), f32),
            pltpu.VMEM((total // 2, EDGE, width), f32),
            pltpu.VMEM((layers, 5, rows, width), f32),
            pltpu.VMEM((layers, 5, 4 * EDGE, width), f32),
            pltpu.VMEM((2, 5, tall, width), f32),
            pltpu.VMEM((3, rows, width), f32),
            pltpu.VMEM((slabs, EDGE, width), f32),
            pltpu.VMEM((slabs, EDGE, width), f32),
            pltpu.VMEM(((slabs + 3) // 4, EDGE, width), f32),
            pltpu.VMEM(((slabs + 3) // 4, EDGE, width), f32),
            pltpu.VMEM((slabs, rows, width), f32),
            pltpu.VMEM((slabs, rows // 4, width), f32),
            pltpu.VMEM((slabs, rows, width), f32),
            pltpu.VMEM((slabs, rows // 4, width), f32),
            pltpu.VMEM((slabs, rows, width), f32),
            dma((4,)), dma((16,)), dma((16,)),
            dma((slabs,)), dma((slabs,)), dma((slabs,)), dma((slabs,)), dma((slabs,)), dma((slabs,)),
        ],
        compiler_params=pltpu.CompilerParams(
            collective_id=0, has_side_effects=True, vmem_limit_bytes=60 * 1024 * 1024
        ),
        cost_estimate=pl.CostEstimate(
            flops=50_000_000, bytes_accessed=800_000, transcendentals=0
        ),
    )(
        fluid_state.reshape(slabs, rows, width),
        velocity.reshape(vels, rows, width),
        shifts.reshape(1, rows),
        fraction.reshape(1, rows),
    )
    return result.reshape(fields, layers, rows, width)


def solution(mesh):
    return jax.shard_map(
        on_device,
        mesh=mesh,
        in_specs=(P(None, None, "rad", "az"), P(None, None, "rad", "az"), P("rad"), P("rad")),
        out_specs=P(None, None, "rad", "az"),
        check_vma=False,
    )
```

```python
import functools

import jax
import jax.numpy as jnp
from jax import lax
from jax.experimental import pallas as pl
from jax.experimental.pallas import tpu as pltpu
from jax.sharding import PartitionSpec as P

STEPS = 2
EDGE = 8
NINE = 9


def kernel(
    n_az, n_rad, fields, layers,
    fluid, vel, shift_hbm, frac_hbm, out,
    shift_ref, frac_ref, shift_b, weight_b, xin, own_lo, own_hi, row_lo, row_hi, halo_l, halo_r, halo_d, halo_u,
    coef, coef_s, coef_t, seam, brim, got_brim, brim_tail, got_brim_tail, rot, tail, got, got_tail, relayed,
    in_sem, send_h, recv_h, send_a, recv_a, send_b, recv_b, send_f, recv_f,
):
    slabs = fields * layers
    vels = 2 * layers
    total = slabs + vels
    rows, width = xin.shape[1], xin.shape[2]
    tall = rows + 2 * EDGE
    az = lax.axis_index("az")
    rad = lax.axis_index("rad")
    right = lax.rem(az + 1, n_az)
    right2 = lax.rem(az + 2, n_az)
    left = lax.rem(az + n_az - 1, n_az)
    left2 = lax.rem(az + n_az - 2, n_az)
    has_dn = rad > 0
    has_up = rad < n_rad - 1

    def dev(a, r):
        return {"az": a, "rad": r}

    barrier = pltpu.get_barrier_semaphore()
    for a in (right, left, left2):
        pl.semaphore_signal(barrier, inc=1, device_id=dev(a, rad))

    @pl.when(has_dn)
    def _():
        for a in (right, left, az):
            pl.semaphore_signal(barrier, inc=1, device_id=dev(a, rad - 1))

    @pl.when(has_up)
    def _():
        for a in (right, left, az):
            pl.semaphore_signal(barrier, inc=1, device_id=dev(a, rad + 1))

    load_f = pltpu.make_async_copy(fluid, xin.at[pl.ds(0, slabs)], in_sem.at[0])
    load_v = pltpu.make_async_copy(vel, xin.at[pl.ds(slabs, vels)], in_sem.at[1])
    load_s = pltpu.make_async_copy(shift_hbm, shift_ref, in_sem.at[2])
    load_w = pltpu.make_async_copy(frac_hbm, frac_ref, in_sem.at[3])
    loads = (load_s, load_w, load_f, load_v)
    for c in loads:
        c.start()

    quarter = width // 4
    rows4 = rows // 4

    def iota(shape, axis):
        return lax.broadcasted_iota(jnp.int32, shape, axis)

    sub8 = iota((EDGE, width), 0)
    lane_r = iota((rows, width), 1)
    half = EDGE // 2
    own = pl.ds(EDGE, rows)

    for c in loads:
        c.wait()

    for i in range(total // 2):
        a, b = xin[2 * i, rows - EDGE :, :], xin[2 * i + 1, rows - EDGE :, :]
        row_hi[i] = jnp.where(sub8 >= half, a, pltpu.roll(b, half, 0))
        a, b = xin[2 * i, :EDGE, :], xin[2 * i + 1, :EDGE, :]
        row_lo[i] = jnp.where(sub8 < half, a, pltpu.roll(b, half, 0))
    lo = xin[0]
    hi = pltpu.roll(xin[0], NINE, 1)
    for j in range(1, total):
        x = xin[j]
        mine = lane_r >= NINE * j
        hi = jnp.where(mine, pltpu.roll(x, (NINE * (j + 1)) % width, 1), hi)
        lo = jnp.where(mine, pltpu.roll(x, NINE * j, 1), lo)
    own_hi[own, :] = hi
    own_lo[own, :] = lo

    def prev(x, axis):
        return pltpu.roll(x, 1, axis)

    def nxt(x, axis):
        return pltpu.roll(x, x.shape[axis] - 1, axis)

    def coefficients(vr, va, keep):
        face_r = 0.5 * (prev(vr, 0) + vr)
        face_a = 0.5 * (prev(va, 1) + va)
        rp, rm = jnp.maximum(face_r, 0.0), jnp.minimum(face_r, 0.0)
        ap, am = jnp.maximum(face_a, 0.0), jnp.minimum(face_a, 0.0)
        mid_c = 1.0 + ((rm - nxt(rp, 0)) + (am - nxt(ap, 1)))
        all5 = [mid_c, rp, -nxt(rm, 0), ap, -nxt(am, 1)]
        if keep is not None:
            all5 = [jnp.where(keep, c, 0.0) for c in all5]
        return all5

    def transport(values, pick):
        def stencil(n, x):
            return (
                (pick(n, 0) * x + pick(n, 1) * prev(x, 0))
                + (pick(n, 2) * nxt(x, 0) + pick(n, 3) * prev(x, 1))
                + pick(n, 4) * nxt(x, 1)
            )

        for _ in range(STEPS):
            once = [stencil(n, x) for n, x in enumerate(values)]
            twice = [stencil(n, x) for n, x in enumerate(once)]
            values = [0.5 * (x + t) for x, t in zip(values, twice)]
        return values

    for layer in range(layers):
        cs = coefficients(xin[slabs + layer], xin[slabs + layers + layer], None)
        for k in range(5):
            coef[layer, k] = cs[k]

    pick_row = iota((rows, rows), 0) == iota((rows, rows), 1)

    def to_rows(ref):
        spread = jnp.broadcast_to(ref[...].astype(jnp.float32), (rows, rows))
        return jnp.sum(jnp.where(pick_row, spread, 0.0), axis=1, keepdims=True)

    shift_b[...] = jnp.broadcast_to(to_rows(shift_ref).astype(jnp.int32), (rows, width))
    weight_b[...] = jnp.broadcast_to(to_rows(frac_ref), (rows, width))

    pl.semaphore_wait(
        barrier, 3 + 3 * has_dn.astype(jnp.int32) + 3 * has_up.astype(jnp.int32)
    )

    def remote(src, dst, k, a, r):
        return pltpu.make_async_remote_copy(
            src_ref=src, dst_ref=dst, send_sem=send_h.at[k], recv_sem=recv_h.at[k],
            device_id=dev(a, r), device_id_type=pl.DeviceIdType.MESH,
        )

    top = pl.ds(rows, EDGE)
    bottom = pl.ds(EDGE, EDGE)
    after = pl.ds(EDGE + rows, EDGE)
    before = pl.ds(0, EDGE)
    to_up = [
        remote(own_hi.at[top], halo_l.at[before], 3, right, rad + 1),
        remote(own_lo.at[top], halo_r.at[before], 4, left, rad + 1),
        remote(own_hi.at[top], own_hi.at[before], 8, az, rad + 1),
        remote(own_lo.at[top], own_lo.at[before], 9, az, rad + 1),
        remote(row_hi, halo_d, 2, az, rad + 1),
    ]
    to_dn = [
        remote(own_hi.at[bottom], halo_l.at[after], 6, right, rad - 1),
        remote(own_lo.at[bottom], halo_r.at[after], 7, left, rad - 1),
        remote(own_hi.at[bottom], own_hi.at[after], 10, az, rad - 1),
        remote(own_lo.at[bottom], own_lo.at[after], 11, az, rad - 1),
        remote(row_lo, halo_u, 5, az, rad - 1),
    ]
    sides = [
        remote(own_hi.at[own], halo_l.at[own], 0, right, rad),
        remote(own_lo.at[own], halo_r.at[own], 1, left, rad),
    ]
    for c in sides:
        c.start()

    @pl.when(has_up)
    def _():
        for c in to_up:
            c.start()

    @pl.when(has_dn)
    def _():
        for c in to_dn:
            c.start()

    def send_a_of(j):
        return pltpu.make_async_remote_copy(
            src_ref=rot.at[j], dst_ref=got.at[j], send_sem=send_a.at[j], recv_sem=recv_a.at[j],
            device_id=dev(right, rad), device_id_type=pl.DeviceIdType.MESH,
        )

    def send_b_of(j):
        return pltpu.make_async_remote_copy(
            src_ref=tail.at[j], dst_ref=got_tail.at[j], send_sem=send_b.at[j], recv_sem=recv_b.at[j],
            device_id=dev(right2, rad), device_id_type=pl.DeviceIdType.MESH,
        )


    even = lax.rem(az, 2) == 0
    is_even = jnp.full((rows, width), lax.rem(az, 2), jnp.int32) == 0

    def relay_of(j):
        return pltpu.make_async_remote_copy(
            src_ref=got.at[j], dst_ref=relayed.at[j], send_sem=send_f.at[j], recv_sem=recv_f.at[j],
            device_id=dev(right, rad), device_id_type=pl.DeviceIdType.MESH,
        )

    def take(x, index):
        return jnp.take_along_axis(x, index, axis=1, mode="promise_in_bounds")

    weight, shift = weight_b[...], shift_b[...]
    source = (lane_r - shift) & (width - 1)
    lane_q = lane_r[:rows4]

    def interior(layer, carry):
        values = [xin[f * layers + layer] for f in range(fields)]
        values = transport(values, lambda n, k: coef[layer, k])
        for f, v in enumerate(values):
            j = f * layers + layer
            y = (1.0 - weight) * v + weight * prev(v, 1)
            turned = take(y, source)
            rot[j] = turned
            send_a_of(j).start()
            packed = turned[:rows4]
            for q in range(1, 4):
                part = pltpu.roll(turned[q * rows4 : (q + 1) * rows4], q * quarter, 1)
                packed = jnp.where(lane_q >= q * quarter, part, packed)
            tail[j] = packed
        return carry

    lax.fori_loop(0, layers, interior, 0)

    corner_up, corner_dn = to_up.pop(1), to_dn.pop(1)
    sides[0].wait_recv()

    @pl.when(has_dn)
    def _():
        for c in to_up:
            c.wait_recv()

    @pl.when(has_up)
    def _():
        for c in to_dn:
            c.wait_recv()

    row_s = iota((4 * EDGE, width), 0)
    keep_s = jnp.logical_and(
        jnp.logical_or(row_s >= EDGE, has_dn), jnp.logical_or(row_s < 3 * EDGE, has_up)
    )

    def strip(j):
        below, above = halo_d[j // 2], halo_u[j // 2]
        if j % 2:
            below, above = pltpu.roll(below, half, 0), pltpu.roll(above, half, 0)
        both = jnp.concatenate([below, xin[j, :EDGE], xin[j, rows - EDGE :], above], axis=0)
        return jnp.where(keep_s, both, 0.0)

    for layer in range(layers):
        cs = coefficients(strip(slabs + layer), strip(slabs + layers + layer), keep_s)
        for k in range(5):
            coef_s[layer, k] = cs[k]

    lane_t = iota((tall, width), 1)
    row_t = iota((tall, width), 0)
    keep_t = jnp.logical_and(
        jnp.logical_or(row_t >= EDGE, has_dn), jnp.logical_or(row_t < EDGE + rows, has_up)
    )
    k32 = lane_t & 31
    group = lane_t >> 5
    layer_of = group & 1
    part_of = group >> 1
    lower = k32 < NINE
    offset = jnp.where(lower, k32, k32 - NINE)
    tiles = (fields + 1) // 2

    def seam_columns(before_ref, after_ref, side):
        def columns(slab):
            index = (NINE * slab + offset) & (width - 1)
            x = jnp.where(lower, take(before_ref[...], index), take(after_ref[...], index))
            return jnp.where(keep_t, x, 0.0)

        cs = coefficients(
            columns(slabs + layer_of), columns(slabs + layers + layer_of), keep_t
        )
        for k in range(5):
            coef_t[side, k] = cs[k]
        cols = [
            columns(jnp.minimum(2 * t + part_of, fields - 1) * layers + layer_of)
            for t in range(tiles)
        ]
        cols = transport(cols, lambda n, k: coef_t[side, k])
        cols_y = []
        for v in cols:
            v, p = v[EDGE : EDGE + rows], prev(v, 1)[EDGE : EDGE + rows]
            cols_y.append((1.0 - weight) * v + weight * p)
        return cols_y

    slab_l = (lane_r * 57) >> 9
    m9 = lane_r - NINE * slab_l
    field_l, layer_l = slab_l // layers, slab_l % layers

    def seam_tile(cols_y, first_k):
        at = (64 * (field_l & 1) + 32 * layer_l + m9 + first_k) & (width - 1)
        x = take(cols_y[tiles - 1], at)
        for t in range(tiles - 2, -1, -1):
            x = jnp.where(field_l < 2 * (t + 1), take(cols_y[t], at), x)
        return x

    seam[0] = seam_tile(seam_columns(halo_l, own_lo, 0), 5)
    late_seam = remote(seam.at[0], seam.at[1], 12, right, rad)
    late_seam.start()

    first = sub8 < half

    def outer(x):
        return jnp.where(first, x[:EDGE], x[rows - EDGE :])

    w8, source8, lane8 = outer(weight), outer(source), iota((EDGE, width), 1)
    shift8 = outer(shift)
    spare = [None] * slabs
    for layer in range(layers):
        js = [f * layers + layer for f in range(fields)]
        values = transport([strip(j) for j in js], lambda n, k: coef_s[layer, k])
        for j, v in zip(js, values):
            p = prev(v, 1)
            v8 = jnp.where(first, v[EDGE : 2 * EDGE], v[2 * EDGE : 3 * EDGE])
            p8 = jnp.where(first, p[EDGE : 2 * EDGE], p[2 * EDGE : 3 * EDGE])
            spare[j] = take((1.0 - w8) * v8 + w8 * p8, source8)
            brim[j] = spare[j]
    groups = (slabs + 3) // 4
    for u in range(groups):
        packed = spare[4 * u]
        for q in range(1, min(4, slabs - 4 * u)):
            packed = jnp.where(
                lane8 >= q * quarter, pltpu.roll(spare[4 * u + q], q * quarter, 1), packed
            )
        brim_tail[u] = packed

    late = [
        remote(brim, got_brim, 13, right, rad),
        remote(brim_tail, got_brim_tail, 15, right2, rad),
    ]
    for c in late:
        c.start()
    late.append(late_seam)

    @pl.when(even)
    def _():
        for j in range(slabs):
            send_b_of(j).start()

    sides[1].wait_recv()

    @pl.when(has_dn)
    def _():
        corner_up.wait_recv()
        for c in to_dn + [corner_dn]:
            c.wait_send()

    @pl.when(has_up)
    def _():
        corner_dn.wait_recv()
        for c in to_up + [corner_up]:
            c.wait_send()

    for c in sides:
        c.wait_send()
    seam[2] = seam_tile(seam_columns(own_hi, halo_r, 1), 0)

    in_strip = jnp.logical_or(source <= 4, source >= width - 4)
    here, next_ = lane_r >= shift, lane_r >= shift - width
    low = source <= 4
    seam_lane = jnp.where(
        low, source + 4, jnp.where(here, source - (width - NINE), source - (width - 4))
    )
    at_end = jnp.logical_and(here, jnp.logical_not(low))
    mine = jnp.logical_or(
        jnp.logical_and(here, low),
        jnp.logical_and(jnp.logical_not(jnp.logical_or(here, low)), next_),
    )
    here8, next8 = lane8 >= shift8, lane8 >= shift8 - width

    def relay(j, carry):
        send_a_of(j).wait_recv()

        @pl.when(even)
        def _():
            relay_of(j).start()

        return carry

    lax.fori_loop(0, slabs, relay, 0)

    def gather(j, carry):
        @pl.when(even)
        def _():
            send_b_of(j).wait_recv()

        @pl.when(jnp.logical_not(even))
        def _():
            relay_of(j).wait_recv()

        b = got_tail[j]
        parts = [b] + [pltpu.roll(b, width - q * quarter, 1) for q in range(1, 4)]
        far = jnp.where(is_even, jnp.concatenate(parts, axis=0), relayed[j])
        out[j] = jnp.where(here, rot[j], jnp.where(next_, got[j], far))
        return carry

    lax.fori_loop(0, slabs, gather, 0)
    for c in late:
        c.wait_recv()

    for j in range(slabs):
        at = (NINE * j + seam_lane) & (width - 1)
        patch = jnp.where(
            mine, take(seam[0], at), jnp.where(at_end, take(seam[2], at), take(seam[1], at))
        )
        q = j % 4
        far8 = got_brim_tail[j // 4]
        if q:
            far8 = pltpu.roll(far8, width - q * quarter, 1)
        rim = jnp.where(here8, brim[j], jnp.where(next8, got_brim[j], far8))
        base = jnp.concatenate(
            [
                jnp.where(first, rim, out[j, :EDGE]),
                out[j, EDGE : rows - EDGE],
                jnp.where(first, out[j, rows - EDGE :], rim),
            ],
            axis=0,
        )
        out[j] = jnp.where(in_strip, patch, base)

    for c in late:
        c.wait_send()

    def drain(j, carry):
        send_a_of(j).wait_send()

        @pl.when(even)
        def _():
            send_b_of(j).wait_send()
            relay_of(j).wait_send()

        return carry

    lax.fori_loop(0, slabs, drain, 0)


def on_device(fluid_state, velocity, shifts, fraction):
    fields, layers, rows, width = fluid_state.shape
    n_az, n_rad = lax.axis_size("az"), lax.axis_size("rad")
    slabs, vels = fields * layers, 2 * layers
    total = slabs + vels
    tall = rows + 2 * EDGE
    f32 = jnp.float32
    dma = pltpu.SemaphoreType.DMA
    hbm = pl.BlockSpec(memory_space=pltpu.HBM)
    vmem = pl.BlockSpec(memory_space=pltpu.VMEM)
    result = pl.pallas_call(
        functools.partial(kernel, n_az, n_rad, fields, layers),
        out_shape=pltpu.VMEM((slabs, rows, width), f32),
        in_specs=[hbm, hbm, hbm, hbm],
        out_specs=vmem,
        scratch_shapes=[
            pltpu.VMEM((1, rows), jnp.int32),
            pltpu.VMEM((1, rows), f32),
            pltpu.VMEM((rows, width), jnp.int32),
            pltpu.VMEM((rows, width), f32),
            pltpu.VMEM((total, rows, width), f32),
            pltpu.VMEM((tall, width), f32),
            pltpu.VMEM((tall, width), f32),
            pltpu.VMEM((total // 2, EDGE, width), f32),
            pltpu.VMEM((total // 2, EDGE, width), f32),
            pltpu.VMEM((tall, width), f32),
            pltpu.VMEM((tall, width), f32),
            pltpu.VMEM((total // 2, EDGE, width), f32),
            pltpu.VMEM((total // 2, EDGE, width), f32),
            pltpu.VMEM((layers, 5, rows, width), f32),
            pltpu.VMEM((layers, 5, 4 * EDGE, width), f32),
            pltpu.VMEM((2, 5, tall, width), f32),
            pltpu.VMEM((3, rows, width), f32),
            pltpu.VMEM((slabs, EDGE, width), f32),
            pltpu.VMEM((slabs, EDGE, width), f32),
            pltpu.VMEM(((slabs + 3) // 4, EDGE, width), f32),
            pltpu.VMEM(((slabs + 3) // 4, EDGE, width), f32),
            pltpu.VMEM((slabs, rows, width), f32),
            pltpu.VMEM((slabs, rows // 4, width), f32),
            pltpu.VMEM((slabs, rows, width), f32),
            pltpu.VMEM((slabs, rows // 4, width), f32),
            pltpu.VMEM((slabs, rows, width), f32),
            dma((4,)), dma((16,)), dma((16,)),
            dma((slabs,)), dma((slabs,)), dma((slabs,)), dma((slabs,)), dma((slabs,)), dma((slabs,)),
        ],
        compiler_params=pltpu.CompilerParams(
            collective_id=0, has_side_effects=True, vmem_limit_bytes=60 * 1024 * 1024
        ),
        cost_estimate=pl.CostEstimate(
            flops=50_000_000, bytes_accessed=800_000, transcendentals=0
        ),
    )(
        fluid_state.reshape(slabs, rows, width),
        velocity.reshape(vels, rows, width),
        shifts.reshape(1, rows),
        fraction.reshape(1, rows),
    )
    return result.reshape(fields, layers, rows, width)


def solution(mesh):
    return jax.shard_map(
        on_device,
        mesh=mesh,
        in_specs=(P(None, None, "rad", "az"), P(None, None, "rad", "az"), P("rad"), P("rad")),
        out_specs=P(None, None, "rad", "az"),
        check_vma=False,
    )
```
